128 devices in a mesh: path: 8 (over z, x_lo), trade: 16 (over x_hi, y, core).
Axes of the slice: x: 4 (x_hi: 2, x_lo: 2; x = x_hi * 2 + x_lo), y: 4, z: 4, core: 2. Of those that a mesh axis runs over, the one named last changes fastest.
Arguments:
- factors: bfloat16 [32, 8, 1024], P(None, None, 'path'), may hold values from -5 to 5
- loadings: bfloat16 [32, 8, 65536], P(None, None, 'trade'), may hold values from -0.5 to 0.5
- notional: float32 [65536], P('trade'), may hold values from -1 to 1
- strike: float32 [65536], P('trade'), may hold values from 0.5 to 1.5
- date_weight: float32 [32], replicated, may hold values from 0.3 to 3
- loss_spanning: float32 [256], replicated, may hold values from 0.2 to 0.9
- loss_local: float32 [2048], P('trade'), may hold values from 0.2 to 0.9
- trade_slot: int32 [65536], P('trade'), may hold values from 0 to 255
- span_list: int32 [2048], P('trade'), may hold values from 0 to 255, as said below
Outputs:
- loading_grad: float32 [32, 8, 65536], P('path', None, 'trade')
- factor_grad: float32 [32, 8, 1024], P('trade', None, 'path')
The draws below stay inside these ranges and needn't reach their ends.
Inputs may be any that keep to these rules, and one draw needn't show every extreme that they name: `trade_slot`: slot s < 128 of a trade shard holds that shard's spanning set from span_list; slot 128 + i holds the shard's i-th local set. `span_list`: the 128 entries of one trade shard are distinct spanning set ids.
All inputs are finite; a program needn't handle non-finite values.
Results may differ from the reference program's by a relative error of at most 0.0021.
Values may be sent and summed in bfloat16 or wider, within the bound.
No kernel may reach another device: no remote copies, remote signals or barrier semaphores. Data moves between devices by JAX's collectives and lax.ppermute only.
A program may use at most 64 MiB of HBM per device.

```python
import math
import jax
import jax.numpy as jnp
import numpy as np
from jax import lax

FACTORS = 8
DATES = 32
K_DEV = 4096
SLOTS = 256
SPAN_DEV = 128
LOC_DEV = 128
SPAN_ALL = 256
TRADES = 65536
PATHS = 1024
N_TRADE = 16


def draw_span_list(key, part):
    shard_keys = jax.random.split(jax.random.fold_in(key, 11), N_TRADE)
    shards = jnp.arange(N_TRADE, dtype=jnp.int32)

    def one_shard(shard_key, shard):
        order = jax.random.permutation(shard_key, SPAN_ALL).astype(jnp.int32)
        wanted = (shard * (SPAN_ALL - 1) // max(N_TRADE - 1, 1)).astype(jnp.int32)
        position = jnp.argmax(order == wanted)
        leading = order[0]
        order = order.at[position].set(leading).at[0].set(wanted)
        return order[:SPAN_DEV]
    return jax.vmap(one_shard)(shard_keys, shards).reshape(N_TRADE * SPAN_DEV)


def with_ends(result, rng, least, high):
    extent = result.shape
    spot = [jax.random.randint(jax.random.fold_in(rng, axis), (), 0, extent[axis]) for axis in range(len(extent))]
    result = result.at[tuple(spot)].set(least)
    longest = extent.index(max(extent))
    spot[longest] = (spot[longest] + 1) % extent[longest]
    return result.at[tuple(spot)].set(high)


def steps_of(key, extent, cuts, smallest, largest):
    level, own = 1.0, jax.random.fold_in(key, 6)
    for dim, blocks in cuts:
        draws = jnp.exp(jax.random.uniform(jax.random.fold_in(own, dim), (blocks,), jnp.float32, smallest / len(cuts), largest / len(cuts)))
        level = level * jnp.repeat(draws, extent[dim] // blocks).reshape([-1 if axis == dim else 1 for axis in range(len(extent))])
    return level


def rank_table(count, skew):
    portions = [(1 << 20) // math.isqrt(rank ** skew) + 1 for rank in range(1, count + 1)]
    deviation = 1 + sum(portions) // (1 << 30)
    return np.cumsum(np.array([max(1, weight // deviation) for weight in portions]))


def ranked(key, dims, amount, skew):
    grid = rank_table(amount, skew)
    ticket = jax.random.randint(jax.random.fold_in(key, 1), dims, 0, int(grid[amount - 1]))
    grade = jnp.searchsorted(jnp.asarray(grid, jnp.int32), ticket, side="right")
    return jax.random.permutation(jax.random.fold_in(key, 2), amount)[grade].astype(jnp.int32)


def normal_values(key, dims, spread, limit, cuts=(), held_as=jnp.bfloat16):
    gain = steps_of(key, dims, cuts, -0.22, 0.18) if cuts else 1.0
    drawn = jax.random.normal(key, dims, jnp.float32) * spread * gain
    return jnp.minimum(jnp.maximum(drawn, -limit), limit).astype(held_as)


def setup_inputs(seed: int = 0) -> dict:
    key_list = jax.random.split(jax.random.key(seed), 10)
    return {
        "factors": normal_values(key_list[0], (DATES, FACTORS, PATHS), 1.0, 5.0, ((2, 8),)),
        "loadings": normal_values(key_list[1], (DATES, FACTORS, TRADES), 0.12, 0.5, ((2, 16),)),
        "notional": jnp.clip(jax.random.uniform(key_list[2], (TRADES,), jnp.float32, -1.0, 1.0) * steps_of(key_list[2], (TRADES,), ((0, 16),), -0.4, 0.0), -1.0, 1.0),
        "strike": jnp.clip(0.5 + 1.0 * jax.random.uniform(key_list[3], (TRADES,), jnp.float32) ** steps_of(key_list[3], (TRADES,), ((0, 16),), -0.2, 0.2), 0.5, 1.5),
        "date_weight": jnp.clip(jnp.exp(jax.random.uniform(key_list[4], (DATES,), jnp.float32, math.log(0.3), math.log(3.0))), 0.3, 3.0),
        "loss_spanning": jnp.clip(jax.random.uniform(key_list[5], (SPAN_ALL,), jnp.float32, 0.2, 0.9), 0.2, 0.9),
        "loss_local": jnp.clip(0.2 + 0.7 * jax.random.uniform(key_list[6], (N_TRADE * LOC_DEV,), jnp.float32) ** steps_of(key_list[6], (N_TRADE * LOC_DEV,), ((0, 16),), -0.2, 0.2), 0.2, 0.9),
        "trade_slot": with_ends(ranked(key_list[7], (TRADES,), SLOTS, 2), jax.random.fold_in(key_list[7], 3), 0, SLOTS - 1).astype(jnp.int32),
        "span_list": draw_span_list(jax.random.fold_in(key_list[9], 71), 0),
    }


smoothing = 0.5


def reference(factors, loadings, notional, strike, date_weight, loss_spanning, loss_local, trade_slot, span_list):
    shard_of = (jnp.arange(TRADES) // K_DEV).astype(jnp.int32)
    global_slot = (shard_of * SLOTS + trade_slot).astype(jnp.int32)
    path_count = factors.shape[2]

    def one_date(date_index):
        factor_now = factors[date_index]
        loading_now = loadings[date_index]
        exponent = jnp.dot(factor_now.T, loading_now, preferred_element_type=jnp.float32)
        growth = jnp.exp(exponent)
        values = (notional[None, :] * (growth - strike[None, :])).astype(jnp.bfloat16)
        partial_sums = jax.ops.segment_sum(values.astype(jnp.float32).T, global_slot, N_TRADE * SLOTS).T
        partial_sums = partial_sums.reshape(path_count, N_TRADE, SLOTS)
        span_part = partial_sums[:, :, :SPAN_DEV].reshape(path_count, N_TRADE * SPAN_DEV)
        span_total = jax.ops.segment_sum(span_part.T, span_list, SPAN_ALL).T
        weight_now = date_weight[date_index]
        span_weight = (weight_now * loss_spanning[None, :] * jax.nn.sigmoid(span_total / smoothing)).astype(jnp.bfloat16)
        local_total = partial_sums[:, :, SPAN_DEV:].reshape(path_count, N_TRADE * LOC_DEV)
        local_weight = (weight_now * loss_local[None, :] * jax.nn.sigmoid(local_total / smoothing)).astype(jnp.bfloat16)
        span_slots = span_weight[:, span_list].reshape(path_count, N_TRADE, SPAN_DEV)
        slot_weight = jnp.concatenate([span_slots, local_weight.reshape(path_count, N_TRADE, LOC_DEV)], axis=2)
        slot_weight = slot_weight.reshape(path_count, N_TRADE * SLOTS)
        trade_weight = slot_weight[:, global_slot].astype(jnp.float32)
        sensitivity = (trade_weight * notional[None, :] * growth).astype(jnp.bfloat16)
        loading_grad = jnp.dot(factor_now, sensitivity, preferred_element_type=jnp.float32) / path_count
        factor_grad = jnp.dot(loading_now, sensitivity.T, preferred_element_type=jnp.float32)
        return loading_grad, factor_grad

    loading_grads, factor_grads = lax.map(one_date, jnp.arange(DATES).astype(jnp.int32))
    return loading_grads, factor_grads
```

```python
import functools
import math

import jax
import jax.numpy as jnp
from jax import lax
from jax.experimental import pallas as pl
from jax.experimental.pallas import tpu as pltpu
from jax.sharding import PartitionSpec as P

smoothing = 0.5
log2e = math.log2(math.e)
f32 = jnp.float32
bf16 = jnp.bfloat16
nt = (((1,), (1,)), ((), ()))


def pieces(x, count):
    parts = []
    for _ in range(count):
        part = lax.reduce_precision(x, 8, 7)
        parts.append(part.astype(bf16))
        x = x - part
    return parts


def split(x):
    high = x.astype(bf16)
    return high, (x - high.astype(f32)).astype(bf16)


def kernel(
    block,
    weight_ref,
    trade_ref,
    column_ref,
    row_ref,
    loss_ref,
    loading_out,
    factor_out,
    values_ref,
    slot_weight_ref,
):
    shards, _, trades = trade_ref.shape
    paths = column_ref.shape[0]
    factors = row_ref.shape[0]
    slots = slot_weight_ref.shape[2]
    span_local = slots // 2
    span_count = loss_ref.shape[1]
    steps = trades // block
    weight = weight_ref[0, 0]
    column = column_ref[...]
    row = row_ref[...]

    def trade_block(shard, step):
        start = pl.multiple_of(step * block, block)
        return trade_ref[shard, :, pl.ds(start, block)].astype(f32)

    def table_of(slot):
        ids = lax.broadcasted_iota(jnp.int32, (slots, block), 0).astype(f32)
        return jnp.where(ids == slot, 1.0, 0.0).astype(bf16)

    def set_table(shard):
        names = trade_ref[shard, :, pl.ds(0, span_local)].astype(f32)[13:14]
        ids = lax.broadcasted_iota(jnp.int32, (span_count, span_local), 0).astype(f32)
        return jnp.where(ids == names, 1.0, 0.0).astype(bf16)

    def forward(shard, span_total):
        def step_of(step, partial):
            data = trade_block(shard, step)
            both = jnp.concatenate(split(data[:8] * log2e), axis=0)
            exponent = jnp.dot(column, both, preferred_element_type=f32)
            notional = data[9:10] + data[10:11]
            strike = data[11:12] + data[12:13]
            values = (notional * (jnp.exp2(exponent) - strike)).astype(bf16)
            start = pl.multiple_of(shard * trades + step * block, block)
            values_ref[:, pl.ds(start, block)] = values
            return partial + lax.dot_general(
                values, table_of(data[8:9]), nt, preferred_element_type=f32
            )

        partial = lax.fori_loop(0, steps, step_of, jnp.zeros((paths, slots), f32))
        loss = trade_ref[shard, :, pl.ds(span_local, 3 * span_local)].astype(f32)[13:14]
        loss = (
            loss[:, :span_local]
            + loss[:, span_local : 2 * span_local]
            + loss[:, 2 * span_local :]
        )
        local = weight * loss * jax.nn.sigmoid(partial[:, span_local:] / smoothing)
        slot_weight_ref[shard, :, span_local:] = local.astype(bf16)
        table = set_table(shard)
        for part in split(partial[:, :span_local]):
            span_total = span_total + lax.dot_general(
                part, table, nt, preferred_element_type=f32
            )
        return span_total

    span_total = lax.fori_loop(0, shards, forward, jnp.zeros((paths, span_count), f32))
    span_weight = (weight * loss_ref[...] * jax.nn.sigmoid(span_total / smoothing)).astype(bf16)

    def backward(shard, total):
        slot_weight_ref[shard, :, :span_local] = jnp.dot(
            span_weight, set_table(shard), preferred_element_type=f32
        ).astype(bf16)

        def step_of(step, total):
            data = trade_block(shard, step)
            table = table_of(data[8:9])
            trade_weight = jnp.dot(slot_weight_ref[shard], table, preferred_element_type=f32)
            notional = data[9:10] + data[10:11]
            strike = data[11:12] + data[12:13]
            start = pl.multiple_of(shard * trades + step * block, block)
            scaled = values_ref[:, pl.ds(start, block)].astype(f32) + notional * strike
            sensitivity = (trade_weight * scaled).astype(bf16)
            start = pl.multiple_of(step * block, block)
            loading_out[shard, :, pl.ds(start, block)] = jnp.dot(
                row, sensitivity, preferred_element_type=f32
            ).astype(bf16)
            return total + lax.dot_general(
                data[:8].astype(bf16), sensitivity, nt, preferred_element_type=f32
            )

        return lax.fori_loop(0, steps, step_of, total)

    factor_out[...] = lax.fori_loop(0, shards, backward, jnp.zeros((factors, paths), f32))


def price_and_adjoint(weight, trade_data, factor_rows, loss_spanning, block=1024):
    shards, _, trades = trade_data.shape
    factors, paths = factor_rows.shape
    slots = 256
    column = jnp.concatenate([factor_rows, factor_rows], axis=0).T
    vmem = pl.BlockSpec(memory_space=pltpu.VMEM)
    return pl.pallas_call(
        functools.partial(kernel, block),
        out_shape=(
            jax.ShapeDtypeStruct((shards, factors, trades), bf16),
            jax.ShapeDtypeStruct((factors, paths), f32),
        ),
        in_specs=[pl.BlockSpec(memory_space=pltpu.SMEM), vmem, vmem, vmem, vmem],
        out_specs=(vmem, vmem),
        scratch_shapes=[
            pltpu.VMEM((paths, shards * trades), bf16),
            pltpu.VMEM((shards, paths, slots), bf16),
        ],
        compiler_params=pltpu.CompilerParams(vmem_limit_bytes=58 * 2**20),
    )(weight, trade_data, column, factor_rows, loss_spanning)


def on_device(
    factors,
    loadings,
    notional,
    strike,
    date_weight,
    loss_spanning,
    loss_local,
    trade_slot,
    span_list,
):
    path_devices = lax.axis_size("path")
    trade_devices = lax.axis_size("trade")
    path_at = lax.axis_index("path")
    trade_at = lax.axis_index("trade")
    dates, factor_count, chunk = factors.shape
    trades = loadings.shape[2]
    group_dates = dates // path_devices
    quarters = trade_devices // group_dates
    span_local = span_list.shape[0]

    own = lax.dynamic_slice_in_dim(loadings, path_at * group_dates, group_dates, 0)
    lists = jnp.concatenate([span_list.astype(bf16)] + pieces(loss_local, 3))
    lists = jnp.concatenate([lists, jnp.zeros((trades - lists.shape[0],), bf16)])
    zero = jnp.zeros((trades,), bf16)
    extra = jnp.stack(
        [trade_slot.astype(bf16)] + pieces(notional, 2) + pieces(strike, 2) + [lists, zero, zero]
    )
    sent = jnp.concatenate(
        [
            jnp.repeat(own, quarters, axis=0),
            jnp.broadcast_to(extra[None], (trade_devices,) + extra.shape),
        ],
        axis=1,
    )
    trade_data = lax.all_to_all(sent, "trade", 0, 0, tiled=True)

    routes = []
    for turn in range(2):
        route = []
        for a in range(path_devices):
            for b in range(trade_devices):
                date = 2 * b + (a + turn) % 2
                to = (date // group_dates) * trade_devices + (date % group_dates) * quarters + a // 2
                route.append((a * trade_devices + b, to))
        routes.append(route)
    mine = lax.dynamic_slice_in_dim(factors, 2 * trade_at, 2, 0)
    odd_path = path_at % 2 == 1
    odd_date = (trade_at // quarters) % 2 == 1
    first = jnp.where(odd_path, mine[1], mine[0])
    second = jnp.where(odd_path, mine[0], mine[1])
    first = lax.ppermute(first, ("path", "trade"), routes[0])
    second = lax.ppermute(second, ("path", "trade"), routes[1])
    factor_rows = jnp.where(
        odd_date,
        jnp.concatenate([second, first], axis=1),
        jnp.concatenate([first, second], axis=1),
    )

    date_at = path_at * group_dates + trade_at // quarters
    weight = lax.dynamic_slice_in_dim(date_weight, date_at, 1).reshape(1, 1)
    loading_part, factor_part = price_and_adjoint(
        weight, trade_data, factor_rows, loss_spanning[None, :]
    )

    back = [[(to, origin) for origin, to in route] for route in routes]
    left, right = factor_part[:, :chunk], factor_part[:, chunk:]
    first = lax.ppermute(jnp.where(odd_date, right, left), ("path", "trade"), back[0])
    second = lax.ppermute(jnp.where(odd_date, left, right), ("path", "trade"), back[1])
    factor_grad = jnp.where(odd_path, jnp.stack([second, first]), jnp.stack([first, second]))

    loading_part = lax.all_to_all(loading_part, "trade", 0, 0, tiled=True)
    loading_part = loading_part.reshape(group_dates, quarters, factor_count, trades)
    loading_grad = loading_part.astype(f32).sum(axis=1) / (path_devices * chunk)
    return (loading_grad, factor_grad)


def solution(mesh):
    return jax.shard_map(
        on_device,
        mesh=mesh,
        in_specs=(
            P(None, None, "path"),
            P(None, None, "trade"),
            P("trade"),
            P("trade"),
            P(),
            P(),
            P("trade"),
            P("trade"),
            P("trade"),
        ),
        out_specs=(P("path", None, "trade"), P("trade", None, "path")),
        check_vma=False,
    )
```

```python
import functools
import math

import jax
import jax.numpy as jnp
from jax import lax
from jax.experimental import pallas as pl
from jax.experimental.pallas import tpu as pltpu
from jax.sharding import PartitionSpec as P

smoothing = 0.5
log2e = math.log2(math.e)
f32 = jnp.float32
bf16 = jnp.bfloat16
nt = (((1,), (1,)), ((), ()))


def pieces(x, count):
    parts = []
    for _ in range(count):
        part = lax.reduce_precision(x, 8, 7)
        parts.append(part.astype(bf16))
        x = x - part
    return parts


def split(x):
    high = x.astype(bf16)
    return high, (x - high.astype(f32)).astype(bf16)


def kernel(
    block,
    weight_ref,
    trade_ref,
    column_ref,
    row_ref,
    loss_ref,
    loading_out,
    factor_out,
    values_ref,
    slot_weight_ref,
):
    shards, _, trades = trade_ref.shape
    paths = column_ref.shape[0]
    factors = row_ref.shape[0]
    slots = slot_weight_ref.shape[2]
    span_local = slots // 2
    span_count = loss_ref.shape[1]
    steps = trades // block
    weight = weight_ref[0, 0]
    column = column_ref[...]
    row = row_ref[...]

    def trade_block(shard, step):
        start = pl.multiple_of(step * block, block)
        return trade_ref[shard, :, pl.ds(start, block)].astype(f32)

    def table_of(slot):
        ids = lax.broadcasted_iota(jnp.int32, (slots, block), 0).astype(f32)
        return jnp.where(ids == slot, 1.0, 0.0).astype(bf16)

    def set_table(shard):
        names = trade_ref[shard, :, pl.ds(0, span_local)].astype(f32)[13:14]
        ids = lax.broadcasted_iota(jnp.int32, (span_count, span_local), 0).astype(f32)
        return jnp.where(ids == names, 1.0, 0.0).astype(bf16)

    def forward(shard, span_total):
        def step_of(step, partial):
            data = trade_block(shard, step)
            both = jnp.concatenate(split(data[:8] * log2e), axis=0)
            exponent = jnp.dot(column, both, preferred_element_type=f32)
            notional = data[9:10] + data[10:11]
            strike = data[11:12] + data[12:13]
            values = (notional * (jnp.exp2(exponent) - strike)).astype(bf16)
            start = pl.multiple_of(shard * trades + step * block, block)
            values_ref[:, pl.ds(start, block)] = values
            return partial + lax.dot_general(
                values, table_of(data[8:9]), nt, preferred_element_type=f32
            )

        partial = lax.fori_loop(0, steps, step_of, jnp.zeros((paths, slots), f32))
        loss = trade_ref[shard, :, pl.ds(span_local, 3 * span_local)].astype(f32)[13:14]
        loss = (
            loss[:, :span_local]
            + loss[:, span_local : 2 * span_local]
            + loss[:, 2 * span_local :]
        )
        local = weight * loss * jax.nn.sigmoid(partial[:, span_local:] / smoothing)
        slot_weight_ref[shard, :, span_local:] = local.astype(bf16)
        table = set_table(shard)
        for part in split(partial[:, :span_local]):
            span_total = span_total + lax.dot_general(
                part, table, nt, preferred_element_type=f32
            )
        return span_total

    span_total = lax.fori_loop(0, shards, forward, jnp.zeros((paths, span_count), f32))
    span_weight = (weight * loss_ref[...] * jax.nn.sigmoid(span_total / smoothing)).astype(bf16)

    def backward(shard, total):
        slot_weight_ref[shard, :, :span_local] = jnp.dot(
            span_weight, set_table(shard), preferred_element_type=f32
        ).astype(bf16)

        def step_of(step, total):
            data = trade_block(shard, step)
            table = table_of(data[8:9])
            trade_weight = jnp.dot(slot_weight_ref[shard], table, preferred_element_type=f32)
            notional = data[9:10] + data[10:11]
            strike = data[11:12] + data[12:13]
            start = pl.multiple_of(shard * trades + step * block, block)
            scaled = values_ref[:, pl.ds(start, block)].astype(f32) + notional * strike
            sensitivity = (trade_weight * scaled).astype(bf16)
            start = pl.multiple_of(step * block, block)
            loading_out[shard, :, pl.ds(start, block)] = jnp.dot(
                row, sensitivity, preferred_element_type=f32
            ).astype(bf16)
            return total + lax.dot_general(
                data[:8].astype(bf16), sensitivity, nt, preferred_element_type=f32
            )

        return lax.fori_loop(0, steps, step_of, total)

    factor_out[...] = lax.fori_loop(0, shards, backward, jnp.zeros((factors, paths), f32))


def price_and_adjoint(weight, trade_data, factor_rows, loss_spanning, block=4096):
    shards, _, trades = trade_data.shape
    factors, paths = factor_rows.shape
    slots = 256
    column = jnp.concatenate([factor_rows, factor_rows], axis=0).T
    vmem = pl.BlockSpec(memory_space=pltpu.VMEM)
    return pl.pallas_call(
        functools.partial(kernel, block),
        out_shape=(
            jax.ShapeDtypeStruct((shards, factors, trades), bf16),
            jax.ShapeDtypeStruct((factors, paths), f32),
        ),
        in_specs=[pl.BlockSpec(memory_space=pltpu.SMEM), vmem, vmem, vmem, vmem],
        out_specs=(vmem, vmem),
        scratch_shapes=[
            pltpu.VMEM((paths, shards * trades), bf16),
            pltpu.VMEM((shards, paths, slots), bf16),
        ],
        compiler_params=pltpu.CompilerParams(vmem_limit_bytes=58 * 2**20),
    )(weight, trade_data, column, factor_rows, loss_spanning)


def on_device(
    factors,
    loadings,
    notional,
    strike,
    date_weight,
    loss_spanning,
    loss_local,
    trade_slot,
    span_list,
):
    path_devices = lax.axis_size("path")
    trade_devices = lax.axis_size("trade")
    path_at = lax.axis_index("path")
    trade_at = lax.axis_index("trade")
    dates, factor_count, chunk = factors.shape
    trades = loadings.shape[2]
    group_dates = dates // path_devices
    quarters = trade_devices // group_dates
    span_local = span_list.shape[0]

    own = lax.dynamic_slice_in_dim(loadings, path_at * group_dates, group_dates, 0)
    lists = jnp.concatenate([span_list.astype(bf16)] + pieces(loss_local, 3))
    lists = jnp.concatenate([lists, jnp.zeros((trades - lists.shape[0],), bf16)])
    zero = jnp.zeros((trades,), bf16)
    extra = jnp.stack(
        [trade_slot.astype(bf16)] + pieces(notional, 2) + pieces(strike, 2) + [lists, zero, zero]
    )
    sent = jnp.concatenate(
        [
            jnp.repeat(own, quarters, axis=0),
            jnp.broadcast_to(extra[None], (trade_devices,) + extra.shape),
        ],
        axis=1,
    )
    trade_data = lax.all_to_all(sent, "trade", 0, 0, tiled=True)

    routes = []
    for turn in range(2):
        route = []
        for a in range(path_devices):
            for b in range(trade_devices):
                date = 2 * b + (a + turn) % 2
                to = (date // group_dates) * trade_devices + (date % group_dates) * quarters + a // 2
                route.append((a * trade_devices + b, to))
        routes.append(route)
    mine = lax.dynamic_slice_in_dim(factors, 2 * trade_at, 2, 0)
    odd_path = path_at % 2 == 1
    odd_date = (trade_at // quarters) % 2 == 1
    first = jnp.where(odd_path, mine[1], mine[0])
    second = jnp.where(odd_path, mine[0], mine[1])
    first = lax.ppermute(first, ("path", "trade"), routes[0])
    second = lax.ppermute(second, ("path", "trade"), routes[1])
    factor_rows = jnp.where(
        odd_date,
        jnp.concatenate([second, first], axis=1),
        jnp.concatenate([first, second], axis=1),
    )

    date_at = path_at * group_dates + trade_at // quarters
    weight = lax.dynamic_slice_in_dim(date_weight, date_at, 1).reshape(1, 1)
    loading_part, factor_part = price_and_adjoint(
        weight, trade_data, factor_rows, loss_spanning[None, :]
    )

    back = [[(to, origin) for origin, to in route] for route in routes]
    left, right = factor_part[:, :chunk], factor_part[:, chunk:]
    first = lax.ppermute(jnp.where(odd_date, right, left), ("path", "trade"), back[0])
    second = lax.ppermute(jnp.where(odd_date, left, right), ("path", "trade"), back[1])
    factor_grad = jnp.where(odd_path, jnp.stack([second, first]), jnp.stack([first, second]))

    loading_part = lax.all_to_all(loading_part, "trade", 0, 0, tiled=True)
    loading_part = loading_part.reshape(group_dates, quarters, factor_count, trades)
    loading_grad = loading_part.astype(f32).sum(axis=1) / (path_devices * chunk)
    return (loading_grad, factor_grad)


def solution(mesh):
    return jax.shard_map(
        on_device,
        mesh=mesh,
        in_specs=(
            P(None, None, "path"),
            P(None, None, "trade"),
            P("trade"),
            P("trade"),
            P(),
            P(),
            P("trade"),
            P("trade"),
            P("trade"),
        ),
        out_specs=(P("path", None, "trade"), P("trade", None, "path")),
        check_vma=False,
    )
```

```python
import functools
import math

import jax
import jax.numpy as jnp
from jax import lax
from jax.experimental import pallas as pl
from jax.experimental.pallas import tpu as pltpu
from jax.sharding import PartitionSpec as P

smoothing = 0.5
log2e = math.log2(math.e)
f32 = jnp.float32
bf16 = jnp.bfloat16
nt = (((1,), (1,)), ((), ()))


def split(x):
    high = x.astype(bf16)
    return high, (x - high.astype(f32)).astype(bf16)


def split3(x):
    high, low = split(x)
    return high, low, split(x - high.astype(f32))[1]


def rows_of(data):
    half = data.shape[1]
    loading = jnp.concatenate([data[0:8], data[8:16]], axis=1)
    slot = jnp.concatenate([data[16:17], data[17:18]], axis=1)
    notional = jnp.concatenate(
        [data[18:19] + data[20:21], data[19:20] + data[21:22]], axis=1
    )
    return loading, slot, notional


def lists_of(data, span_local, slots):
    line = data[22:23]
    local = slots - span_local
    ends = [span_local]
    for width in (local, local, local, slots, slots, slots):
        ends.append(ends[-1] + width)
    part = [line[:, lo:hi] for lo, hi in zip([0] + ends, ends)]
    return part[0], part[1] + part[2] + part[3], part[4] + part[5] + part[6]


def pack_kernel(
    slots, first_ref, loading_ref, notional_ref, strike_ref, slot_ref, span_ref, loss_ref, sent_ref, own_ref, sem
):
    devices, _, half = sent_ref.shape
    group_dates = own_ref.shape[0]
    own = pltpu.make_async_copy(
        loading_ref.at[pl.ds(first_ref[0, 0], group_dates)], own_ref, sem
    )
    own.start()
    trades = notional_ref.shape[1]
    notional = notional_ref[...]
    slot = slot_ref[...].astype(f32)
    amount = notional * (1.0 - strike_ref[...])
    ids = lax.broadcasted_iota(jnp.int32, (slots, trades), 0).astype(f32)
    constant = jnp.where(ids == slot, amount, 0.0).sum(axis=1, keepdims=True)
    constant = jnp.broadcast_to(constant, (slots, 128)).T[0:1]
    lists = [span_ref[...].astype(f32)]
    for values in (loss_ref[...], constant):
        lists += [part.astype(f32) for part in split3(values)]
    lists = jnp.concatenate(lists, axis=1)
    lists = jnp.concatenate([lists, jnp.zeros((1, half - lists.shape[1]), f32)], axis=1)
    high, low = (part.astype(f32) for part in split(notional))
    extra = jnp.concatenate(
        [
            row[:, start : start + half]
            for row in (slot, high, low)
            for start in (0, half)
        ]
        + [lists, jnp.zeros((1, half), f32)],
        axis=0,
    )
    own.wait()
    for date in range(group_dates):
        loading = own_ref[date].astype(f32)
        block = jnp.concatenate([loading[:, :half], loading[:, half:], extra], axis=0).astype(bf16)
        for quarter in range(devices // group_dates):
            sent_ref[date * (devices // group_dates) + quarter] = block


def table_of(slot, slots):
    ids = lax.broadcasted_iota(jnp.int32, (slots, slot.shape[1]), 0).astype(f32)
    return jnp.where(ids == slot, 1.0, 0.0).astype(bf16)


def kernel(
    weight_ref,
    trade_ref,
    column_ref,
    row_ref,
    loss_ref,
    loading_out,
    sensitivity_out,
    values_ref,
    slot_weight_ref,
    sems,
):
    shards, _, half = trade_ref.shape
    trades = 2 * half
    paths = column_ref.shape[0]
    slots = slot_weight_ref.shape[2]
    span_local = slots // 2
    span_count = loss_ref.shape[1]
    weight = weight_ref[0, 0]
    column = column_ref[...]
    row = row_ref[...]

    def place(shard):
        return pl.ds(pl.multiple_of(shard * trades, trades), trades)

    def forward(shard, span_total):
        data = trade_ref[shard].astype(f32)
        loading, slot, notional = rows_of(data)
        names, loss, constant = lists_of(data, span_local, slots)
        both = jnp.concatenate(split(loading * log2e), axis=0)
        exponent = jnp.dot(column, both, preferred_element_type=f32)
        values = (notional * (jnp.exp2(exponent) - 1.0)).astype(bf16)
        values_ref[:, place(shard)] = values
        partial = constant + lax.dot_general(
            values, table_of(slot, slots), nt, preferred_element_type=f32
        )
        local = weight * loss * jax.nn.sigmoid(partial[:, span_local:] / smoothing)
        slot_weight_ref[shard, :, span_local:] = local.astype(bf16)
        table = table_of(names, span_count)
        for part in split(partial[:, :span_local]):
            span_total = span_total + lax.dot_general(
                part, table, nt, preferred_element_type=f32
            )
        return span_total

    span_total = lax.fori_loop(0, shards, forward, jnp.zeros((paths, span_count), f32))
    span_weight = (weight * loss_ref[...] * jax.nn.sigmoid(span_total / smoothing)).astype(bf16)

    def copy_out(shard):
        return pltpu.make_async_copy(
            values_ref.at[:, place(shard)], sensitivity_out.at[:, place(shard)], sems.at[shard]
        )

    def backward(shard, carry):
        data = trade_ref[shard].astype(f32)
        _, slot, notional = rows_of(data)
        names, _, _ = lists_of(data, span_local, slots)
        slot_weight_ref[shard, :, :span_local] = jnp.dot(
            span_weight, table_of(names, span_count), preferred_element_type=f32
        ).astype(bf16)
        trade_weight = jnp.dot(
            slot_weight_ref[shard], table_of(slot, slots), preferred_element_type=f32
        )
        scaled = values_ref[:, place(shard)].astype(f32) + notional
        sensitivity = (trade_weight * scaled).astype(bf16)
        values_ref[:, place(shard)] = sensitivity
        copy_out(shard).start()
        loading_out[shard] = jnp.dot(row, sensitivity, preferred_element_type=f32).astype(bf16)
        return carry

    lax.fori_loop(0, shards, backward, 0)

    def drain(shard, carry):
        copy_out(shard).wait()
        return carry

    lax.fori_loop(0, shards, drain, 0)


def factor_kernel(trade_ref, sensitivity_ref, factor_out):
    @pl.when(pl.program_id(0) == 0)
    def _():
        factor_out[...] = jnp.zeros_like(factor_out)

    loading, _, _ = rows_of(trade_ref[0].astype(f32))
    factor_out[...] += lax.dot_general(
        loading.astype(bf16), sensitivity_ref[...], nt, preferred_element_type=f32
    )


vmem = pl.BlockSpec(memory_space=pltpu.VMEM)
smem = pl.BlockSpec(memory_space=pltpu.SMEM)
params = pltpu.CompilerParams(vmem_limit_bytes=58 * 2**20)


def pack(first, loadings, notional, strike, trade_slot, span_list, loss_local, devices, group_dates):
    factors, trades = loadings.shape[1:]
    slots = span_list.shape[0] + loss_local.shape[0]
    return pl.pallas_call(
        functools.partial(pack_kernel, slots),
        out_shape=jax.ShapeDtypeStruct((devices, 24, trades // 2), bf16),
        in_specs=[smem, pl.BlockSpec(memory_space=pl.ANY)] + [vmem] * 5,
        out_specs=vmem,
        scratch_shapes=[
            pltpu.VMEM((group_dates, factors, trades), bf16),
            pltpu.SemaphoreType.DMA,
        ],
        compiler_params=params,
    )(
        first,
        loadings,
        notional[None],
        strike[None],
        trade_slot[None],
        span_list[None],
        loss_local[None],
    )


def price_and_adjoint(weight, trade_data, factor_rows, loss_spanning, slots=256):
    shards, _, half = trade_data.shape
    trades = 2 * half
    factors, paths = factor_rows.shape
    column = jnp.concatenate([factor_rows, factor_rows], axis=0).T
    return pl.pallas_call(
        kernel,
        out_shape=(
            jax.ShapeDtypeStruct((shards, factors, trades), bf16),
            jax.ShapeDtypeStruct((paths, shards * trades), bf16),
        ),
        in_specs=[smem, vmem, vmem, vmem, vmem],
        out_specs=(vmem, pl.BlockSpec(memory_space=pl.ANY)),
        scratch_shapes=[
            pltpu.VMEM((paths, shards * trades), bf16),
            pltpu.VMEM((shards, paths, slots), bf16),
            pltpu.SemaphoreType.DMA((shards,)),
        ],
        compiler_params=params,
        cost_estimate=pl.CostEstimate(
            flops=shards * trades * paths * 2 * 256 * 4,
            bytes_accessed=shards * trades * paths * 2,
            transcendentals=shards * trades * paths,
        ),
    )(weight, trade_data, column, factor_rows, loss_spanning)


def factor_sums(trade_data, sensitivity):
    shards, rows, half = trade_data.shape
    paths, trades = sensitivity.shape[0], 2 * half
    return pl.pallas_call(
        factor_kernel,
        grid=(shards,),
        out_shape=jax.ShapeDtypeStruct((8, paths), f32),
        in_specs=[
            pl.BlockSpec((1, rows, half), lambda shard: (shard, 0, 0)),
            pl.BlockSpec((paths, trades), lambda shard: (0, shard)),
        ],
        out_specs=pl.BlockSpec((8, paths), lambda shard: (0, 0)),
        compiler_params=params,
        cost_estimate=pl.CostEstimate(
            flops=shards * trades * paths * 2 * 256,
            bytes_accessed=shards * trades * paths * 2,
            transcendentals=0,
        ),
    )(trade_data, sensitivity)


def on_device(
    factors,
    loadings,
    notional,
    strike,
    date_weight,
    loss_spanning,
    loss_local,
    trade_slot,
    span_list,
):
    path_devices = lax.axis_size("path")
    trade_devices = lax.axis_size("trade")
    path_at = lax.axis_index("path")
    trade_at = lax.axis_index("trade")
    dates, factor_count, chunk = factors.shape
    trades = loadings.shape[2]
    group_dates = dates // path_devices
    quarters = trade_devices // group_dates

    first_date = (path_at * group_dates).astype(jnp.int32).reshape(1, 1)
    sent = pack(
        first_date,
        loadings,
        notional,
        strike,
        trade_slot,
        span_list,
        loss_local,
        trade_devices,
        group_dates,
    )
    trade_data = lax.all_to_all(sent, "trade", 0, 0, tiled=True)

    routes = []
    for turn in range(2):
        route = []
        for a in range(path_devices):
            for b in range(trade_devices):
                date = 2 * b + (a + turn) % 2
                to = (date // group_dates) * trade_devices + (date % group_dates) * quarters + a // 2
                route.append((a * trade_devices + b, to))
        routes.append(route)
    mine = lax.dynamic_slice_in_dim(factors, 2 * trade_at, 2, 0)
    odd_path = path_at % 2 == 1
    odd_date = (trade_at // quarters) % 2 == 1
    first = jnp.where(odd_path, mine[1], mine[0])
    second = jnp.where(odd_path, mine[0], mine[1])
    first = lax.ppermute(first, ("path", "trade"), routes[0])
    second = lax.ppermute(second, ("path", "trade"), routes[1])
    factor_rows = jnp.where(
        odd_date,
        jnp.concatenate([second, first], axis=1),
        jnp.concatenate([first, second], axis=1),
    )

    date_at = path_at * group_dates + trade_at // quarters
    weight = lax.dynamic_slice_in_dim(date_weight, date_at, 1).reshape(1, 1)
    loading_part, sensitivity = price_and_adjoint(
        weight, trade_data, factor_rows, loss_spanning[None, :]
    )
    loading_part = lax.all_to_all(loading_part, "trade", 0, 0, tiled=True)
    factor_part = factor_sums(trade_data, sensitivity)

    back = [[(to, origin) for origin, to in route] for route in routes]
    left, right = factor_part[:, :chunk], factor_part[:, chunk:]
    first = lax.ppermute(jnp.where(odd_date, right, left), ("path", "trade"), back[0])
    second = lax.ppermute(jnp.where(odd_date, left, right), ("path", "trade"), back[1])
    factor_grad = jnp.where(odd_path, jnp.stack([second, first]), jnp.stack([first, second]))

    loading_part = loading_part.reshape(group_dates, quarters, factor_count, trades)
    loading_grad = loading_part.astype(f32).sum(axis=1) / (path_devices * chunk)
    return (loading_grad, factor_grad)


def solution(mesh):
    return jax.shard_map(
        on_device,
        mesh=mesh,
        in_specs=(
            P(None, None, "path"),
            P(None, None, "trade"),
            P("trade"),
            P("trade"),
            P(),
            P(),
            P("trade"),
            P("trade"),
            P("trade"),
        ),
        out_specs=(P("path", None, "trade"), P("trade", None, "path")),
        check_vma=False,
    )
```

```python
import functools
import math

import jax
import jax.numpy as jnp
from jax import lax
from jax.experimental import pallas as pl
from jax.experimental.pallas import tpu as pltpu
from jax.sharding import PartitionSpec as P

smoothing = 0.5
log2e = math.log2(math.e)
f32 = jnp.float32
bf16 = jnp.bfloat16
nt = (((1,), (1,)), ((), ()))


def split(x):
    high = x.astype(bf16)
    return high, (x - high.astype(f32)).astype(bf16)


def split3(x):
    high, low = split(x)
    return high, low, split(x - high.astype(f32))[1]


def rows_of(data):
    half = data.shape[1]
    loading = jnp.concatenate([data[0:8], data[8:16]], axis=1)
    slot = jnp.concatenate([data[16:17], data[17:18]], axis=1)
    notional = jnp.concatenate(
        [data[18:19] + data[20:21], data[19:20] + data[21:22]], axis=1
    )
    return loading, slot, notional


def lists_of(data, span_local, slots):
    line = data[22:23]
    local = slots - span_local
    ends = [span_local]
    for width in (local, local, local, slots, slots, slots):
        ends.append(ends[-1] + width)
    part = [line[:, lo:hi] for lo, hi in zip([0] + ends, ends)]
    return part[0], part[1] + part[2] + part[3], part[4] + part[5] + part[6]


def pack_kernel(
    slots, first_ref, loading_ref, notional_ref, strike_ref, slot_ref, span_ref, loss_ref, sent_ref, own_ref, sem
):
    devices, _, half = sent_ref.shape
    group_dates = own_ref.shape[0]
    own = pltpu.make_async_copy(
        loading_ref.at[pl.ds(first_ref[0, 0], group_dates)], own_ref, sem
    )
    own.start()
    trades = notional_ref.shape[1]
    notional = notional_ref[...]
    slot = slot_ref[...].astype(f32)
    amount = notional * (1.0 - strike_ref[...])
    ids = lax.broadcasted_iota(jnp.int32, (slots, trades), 0).astype(f32)
    constant = jnp.where(ids == slot, amount, 0.0).sum(axis=1, keepdims=True)
    constant = jnp.broadcast_to(constant, (slots, 128)).T[0:1]
    lists = [span_ref[...].astype(f32)]
    for values in (loss_ref[...], constant):
        lists += [part.astype(f32) for part in split3(values)]
    lists = jnp.concatenate(lists, axis=1)
    lists = jnp.concatenate([lists, jnp.zeros((1, half - lists.shape[1]), f32)], axis=1)
    high, low = (part.astype(f32) for part in split(notional))
    extra = jnp.concatenate(
        [
            row[:, start : start + half]
            for row in (slot, high, low)
            for start in (0, half)
        ]
        + [lists, jnp.zeros((1, half), f32)],
        axis=0,
    )
    own.wait()
    for date in range(group_dates):
        loading = own_ref[date].astype(f32)
        block = jnp.concatenate([loading[:, :half], loading[:, half:], extra], axis=0).astype(bf16)
        for quarter in range(devices // group_dates):
            sent_ref[date * (devices // group_dates) + quarter] = block


def table_of(slot, slots):
    ids = lax.broadcasted_iota(jnp.int32, (slots, slot.shape[1]), 0).astype(f32)
    return jnp.where(ids == slot, 1.0, 0.0).astype(bf16)


def kernel(
    weight_ref,
    trade_ref,
    row_ref,
    loss_ref,
    loading_out,
    factor_out,
    values_ref,
    slot_weight_ref,
):
    shards, _, half = trade_ref.shape
    trades = 2 * half
    factors, paths = row_ref.shape
    slots = slot_weight_ref.shape[2]
    span_local = slots // 2
    span_count = loss_ref.shape[1]
    weight = weight_ref[0, 0]
    row = row_ref[...]
    column = jnp.concatenate([row.astype(f32)] * 2, axis=0).T.astype(bf16)

    def place(shard):
        return pl.ds(pl.multiple_of(shard * trades, trades), trades)

    def forward(shard, span_total):
        data = trade_ref[shard].astype(f32)
        loading, slot, notional = rows_of(data)
        names, loss, constant = lists_of(data, span_local, slots)
        both = jnp.concatenate(split(loading * log2e), axis=0)
        exponent = jnp.dot(column, both, preferred_element_type=f32)
        values = (notional * (jnp.exp2(exponent) - 1.0)).astype(bf16)
        values_ref[:, place(shard)] = values
        partial = constant + lax.dot_general(
            values, table_of(slot, slots), nt, preferred_element_type=f32
        )
        local = weight * loss * jax.nn.sigmoid(partial[:, span_local:] / smoothing)
        slot_weight_ref[shard, :, span_local:] = local.astype(bf16)
        table = table_of(names, span_count)
        for part in split(partial[:, :span_local]):
            span_total = span_total + lax.dot_general(
                part, table, nt, preferred_element_type=f32
            )
        return span_total

    span_total = lax.fori_loop(0, shards, forward, jnp.zeros((paths, span_count), f32))
    span_weight = (weight * loss_ref[...] * jax.nn.sigmoid(span_total / smoothing)).astype(bf16)

    def backward(shard, total):
        data = trade_ref[shard].astype(f32)
        loading, slot, notional = rows_of(data)
        names, _, _ = lists_of(data, span_local, slots)
        slot_weight_ref[shard, :, :span_local] = jnp.dot(
            span_weight, table_of(names, span_count), preferred_element_type=f32
        ).astype(bf16)
        trade_weight = jnp.dot(
            slot_weight_ref[shard], table_of(slot, slots), preferred_element_type=f32
        )
        scaled = values_ref[:, place(shard)].astype(f32) + notional
        sensitivity = (trade_weight * scaled).astype(bf16)
        loading_out[shard] = jnp.dot(row, sensitivity, preferred_element_type=f32).astype(bf16)
        return total + lax.dot_general(
            loading.astype(bf16), sensitivity, nt, preferred_element_type=f32
        )

    factor_out[...] = lax.fori_loop(0, shards, backward, jnp.zeros((factors, paths), f32))


vmem = pl.BlockSpec(memory_space=pltpu.VMEM)
smem = pl.BlockSpec(memory_space=pltpu.SMEM)
params = pltpu.CompilerParams(vmem_limit_bytes=58 * 2**20)


def pack(first, loadings, notional, strike, trade_slot, span_list, loss_local, devices, group_dates):
    factors, trades = loadings.shape[1:]
    slots = span_list.shape[0] + loss_local.shape[0]
    return pl.pallas_call(
        functools.partial(pack_kernel, slots),
        out_shape=jax.ShapeDtypeStruct((devices, 24, trades // 2), bf16),
        in_specs=[smem, pl.BlockSpec(memory_space=pl.ANY)] + [vmem] * 5,
        out_specs=vmem,
        scratch_shapes=[
            pltpu.VMEM((group_dates, factors, trades), bf16),
            pltpu.SemaphoreType.DMA,
        ],
        compiler_params=params,
    )(
        first,
        loadings,
        notional[None],
        strike[None],
        trade_slot[None],
        span_list[None],
        loss_local[None],
    )


def price_and_adjoint(weight, trade_data, factor_rows, loss_spanning, slots=256):
    shards, _, half = trade_data.shape
    trades = 2 * half
    factors, paths = factor_rows.shape
    return pl.pallas_call(
        kernel,
        out_shape=(
            jax.ShapeDtypeStruct((shards, factors, trades), bf16),
            jax.ShapeDtypeStruct((factors, paths), f32),
        ),
        in_specs=[smem, vmem, vmem, vmem],
        out_specs=(vmem, vmem),
        scratch_shapes=[
            pltpu.VMEM((paths, shards * trades), bf16),
            pltpu.VMEM((shards, paths, slots), bf16),
        ],
        compiler_params=params,
        cost_estimate=pl.CostEstimate(
            flops=shards * trades * paths * 2 * 256 * 4,
            bytes_accessed=shards * trades * paths * 2,
            transcendentals=shards * trades * paths,
        ),
    )(weight, trade_data, factor_rows, loss_spanning)


def on_device(
    factors,
    loadings,
    notional,
    strike,
    date_weight,
    loss_spanning,
    loss_local,
    trade_slot,
    span_list,
):
    path_devices = lax.axis_size("path")
    trade_devices = lax.axis_size("trade")
    path_at = lax.axis_index("path")
    trade_at = lax.axis_index("trade")
    dates, factor_count, chunk = factors.shape
    trades = loadings.shape[2]
    group_dates = dates // path_devices
    quarters = trade_devices // group_dates

    first_date = (path_at * group_dates).astype(jnp.int32).reshape(1, 1)
    sent = pack(
        first_date,
        loadings,
        notional,
        strike,
        trade_slot,
        span_list,
        loss_local,
        trade_devices,
        group_dates,
    )
    trade_data = lax.all_to_all(sent, "trade", 0, 0, tiled=True)

    routes = []
    for turn in range(2):
        route = []
        for a in range(path_devices):
            for b in range(trade_devices):
                date = 2 * b + (a + turn) % 2
                to = (date // group_dates) * trade_devices + (date % group_dates) * quarters + a // 2
                route.append((a * trade_devices + b, to))
        routes.append(route)
    mine = lax.dynamic_slice_in_dim(factors, 2 * trade_at, 2, 0)
    odd_path = path_at % 2 == 1
    odd_date = (trade_at // quarters) % 2 == 1
    first = jnp.where(odd_path, mine[1], mine[0])
    second = jnp.where(odd_path, mine[0], mine[1])
    first = lax.ppermute(first, ("path", "trade"), routes[0])
    second = lax.ppermute(second, ("path", "trade"), routes[1])
    factor_rows = jnp.where(
        odd_date,
        jnp.concatenate([second, first], axis=1),
        jnp.concatenate([first, second], axis=1),
    )

    date_at = path_at * group_dates + trade_at // quarters
    weight = lax.dynamic_slice_in_dim(date_weight, date_at, 1).reshape(1, 1)
    loading_part, factor_part = price_and_adjoint(
        weight, trade_data, factor_rows, loss_spanning[None, :]
    )
    loading_part = lax.all_to_all(loading_part, "trade", 0, 0, tiled=True)
    back = [[(to, origin) for origin, to in route] for route in routes]
    left, right = factor_part[:, :chunk], factor_part[:, chunk:]
    first = lax.ppermute(jnp.where(odd_date, right, left), ("path", "trade"), back[0])
    second = lax.ppermute(jnp.where(odd_date, left, right), ("path", "trade"), back[1])
    factor_grad = jnp.where(odd_path, jnp.stack([second, first]), jnp.stack([first, second]))

    loading_part = loading_part.reshape(group_dates, quarters, factor_count, trades)
    loading_grad = loading_part.astype(f32).sum(axis=1) / (path_devices * chunk)
    return (loading_grad, factor_grad)


def solution(mesh):
    return jax.shard_map(
        on_device,
        mesh=mesh,
        in_specs=(
            P(None, None, "path"),
            P(None, None, "trade"),
            P("trade"),
            P("trade"),
            P(),
            P(),
            P("trade"),
            P("trade"),
            P("trade"),
        ),
        out_specs=(P("path", None, "trade"), P("trade", None, "path")),
        check_vma=False,
    )
```

```python
import functools
import math

import jax
import jax.numpy as jnp
from jax import lax
from jax.experimental import pallas as pl
from jax.experimental.pallas import tpu as pltpu
from jax.sharding import PartitionSpec as P

smoothing = 0.5
log2e = math.log2(math.e)
f32 = jnp.float32
bf16 = jnp.bfloat16
nt = (((1,), (1,)), ((), ()))


def split(x):
    high = x.astype(bf16)
    return high, (x - high.astype(f32)).astype(bf16)


def split3(x):
    high, low = split(x)
    return high, low, split(x - high.astype(f32))[1]


def folded(row):
    width = row.shape[1] // 8
    return jnp.concatenate([row[:, at * width : (at + 1) * width] for at in range(8)], axis=0)


def unfolded(block):
    return jnp.concatenate([block[at : at + 1] for at in range(8)], axis=1)


def rows_of(data, trades):
    width = trades // 8
    slot, high, low = (data[:, trades + at * width : trades + (at + 1) * width] for at in range(3))
    return data[:, :trades], unfolded(slot), unfolded(high + low)


def lists_of(data):
    lists = data[:, data.shape[1] - 128 :]
    constant = lists[4:6] + lists[6:8]
    constant = jnp.concatenate([constant[0:1], constant[1:2]], axis=1)
    return lists[0:1], lists[1:2] + lists[2:3] + lists[3:4], constant


def pack_kernel(
    slots, first_ref, loading_ref, notional_ref, strike_ref, slot_ref, span_ref, loss_ref, sent_ref, own_ref, sem
):
    devices = sent_ref.shape[0]
    group_dates = own_ref.shape[0]
    quarters = devices // group_dates
    own = pltpu.make_async_copy(
        loading_ref.at[pl.ds(first_ref[0, 0], group_dates)], own_ref, sem
    )
    own.start()
    trades = notional_ref.shape[1]
    notional = notional_ref[...]
    slot = slot_ref[...].astype(f32)
    amount = notional * (1.0 - strike_ref[...])
    ids = lax.broadcasted_iota(jnp.int32, (slots, trades), 0).astype(f32)
    constant = jnp.where(ids == slot, amount, 0.0).sum(axis=1, keepdims=True)
    constant = jnp.broadcast_to(constant, (slots, 128)).T[0:1]
    lists = [span_ref[...].astype(f32)] + [part.astype(f32) for part in split3(loss_ref[...])]
    for part in split(constant):
        part = part.astype(f32)
        lists += [part[:, : slots // 2], part[:, slots // 2 :]]
    high, low = (part.astype(f32) for part in split(notional))
    extra = [folded(row) for row in (slot, high, low)] + [jnp.concatenate(lists, axis=0)]
    own.wait()
    for date in range(group_dates):
        block = jnp.concatenate([own_ref[date].astype(f32)] + extra, axis=1).astype(bf16)
        for quarter in range(quarters):
            sent_ref[date * quarters + quarter] = block


def table_of(slot, slots):
    ids = lax.broadcasted_iota(jnp.int32, (slots, slot.shape[1]), 0).astype(f32).astype(bf16)
    return jnp.where(ids == slot.astype(bf16), jnp.ones((), bf16), jnp.zeros((), bf16))


def kernel(
    scale,
    weight_ref,
    trade_in,
    row_ref,
    loss_ref,
    loading_out,
    factor_out,
    values_ref,
    slot_weight_ref,
    trade_ref,
    loading_ref,
    trade_sem,
    loading_sem,
):
    shards, _, width = trade_ref.shape
    trades = loading_ref.shape[2]
    factors, paths = row_ref.shape
    slots = slot_weight_ref.shape[2]
    span_local = slots // 2
    span_count = loss_ref.shape[1]
    weight = weight_ref[0, 0]
    row = row_ref[...]
    column = jnp.concatenate([row.astype(f32)] * 2, axis=0).T.astype(bf16)

    def place(shard):
        return pl.ds(pl.multiple_of(shard * trades, trades), trades)

    def copy_in(shard):
        return pltpu.make_async_copy(trade_in.at[shard], trade_ref.at[shard], trade_sem.at[shard])

    def copy_out(shard):
        return pltpu.make_async_copy(
            loading_ref.at[shard], loading_out.at[shard], loading_sem.at[shard]
        )

    def fetch(shard, carry):
        copy_in(shard).start()
        return carry

    lax.fori_loop(0, shards, fetch, 0)

    def forward(shard, span_total):
        copy_in(shard).wait()
        data = trade_ref[shard].astype(f32)
        loading, slot, notional = rows_of(data, trades)
        names, loss, constant = lists_of(data)
        both = jnp.concatenate(split(loading * log2e), axis=0)
        exponent = jnp.dot(column, both, preferred_element_type=f32)
        values = (notional * (jnp.exp2(exponent) - 1.0)).astype(bf16)
        values_ref[:, place(shard)] = values
        partial = constant + lax.dot_general(
            values, table_of(slot, slots), nt, preferred_element_type=f32
        )
        local = weight * loss * jax.nn.sigmoid(partial[:, span_local:] / smoothing)
        slot_weight_ref[shard, :, span_local:] = local.astype(bf16)
        table = table_of(names, span_count)
        for part in split(partial[:, :span_local]):
            span_total = span_total + lax.dot_general(
                part, table, nt, preferred_element_type=f32
            )
        return span_total

    span_total = lax.fori_loop(0, shards, forward, jnp.zeros((paths, span_count), f32), unroll=4)
    span_weight = (weight * loss_ref[...] * jax.nn.sigmoid(span_total / smoothing)).astype(bf16)

    def backward(shard, total):
        data = trade_ref[shard].astype(f32)
        loading, slot, notional = rows_of(data, trades)
        names, _, _ = lists_of(data)
        slot_weight_ref[shard, :, :span_local] = jnp.dot(
            span_weight, table_of(names, span_count), preferred_element_type=f32
        ).astype(bf16)
        trade_weight = jnp.dot(
            slot_weight_ref[shard], table_of(slot, slots), preferred_element_type=f32
        )
        scaled = values_ref[:, place(shard)].astype(f32) + notional
        sensitivity = (trade_weight * scaled).astype(bf16)
        paths_sum = jnp.dot(row, sensitivity, preferred_element_type=f32)
        loading_ref[shard] = (paths_sum * scale).astype(bf16)
        copy_out(shard).start()
        return total + lax.dot_general(
            loading.astype(bf16), sensitivity, nt, preferred_element_type=f32
        )

    factor_out[...] = lax.fori_loop(0, shards, backward, jnp.zeros((factors, paths), f32))

    def drain(shard, carry):
        copy_out(shard).wait()
        return carry

    lax.fori_loop(0, shards, drain, 0)


vmem = pl.BlockSpec(memory_space=pltpu.VMEM)
anywhere = pl.BlockSpec(memory_space=pl.ANY)
smem = pl.BlockSpec(memory_space=pltpu.SMEM)
params = pltpu.CompilerParams(vmem_limit_bytes=58 * 2**20)


def pack(first, loadings, notional, strike, trade_slot, span_list, loss_local, devices, group_dates):
    factors, trades = loadings.shape[1:]
    slots = span_list.shape[0] + loss_local.shape[0]
    return pl.pallas_call(
        functools.partial(pack_kernel, slots),
        out_shape=jax.ShapeDtypeStruct((devices, factors, trades + 3 * (trades // 8) + 128), bf16),
        in_specs=[smem, anywhere] + [vmem] * 5,
        out_specs=vmem,
        scratch_shapes=[
            pltpu.VMEM((group_dates, factors, trades), bf16),
            pltpu.SemaphoreType.DMA,
        ],
        compiler_params=params,
    )(
        first,
        loadings,
        notional[None],
        strike[None],
        trade_slot[None],
        span_list[None],
        loss_local[None],
    )


def price_and_adjoint(weight, trade_data, factor_rows, loss_spanning, trades, slots, scale):
    shards = trade_data.shape[0]
    factors, paths = factor_rows.shape
    return pl.pallas_call(
        functools.partial(kernel, scale),
        out_shape=(
            jax.ShapeDtypeStruct((shards, factors, trades), bf16),
            jax.ShapeDtypeStruct((factors, paths), f32),
        ),
        in_specs=[smem, pl.BlockSpec(memory_space=pltpu.HBM), vmem, vmem],
        out_specs=(anywhere, vmem),
        scratch_shapes=[
            pltpu.VMEM((paths, shards * trades), bf16),
            pltpu.VMEM((shards, paths, slots), bf16),
            pltpu.VMEM(trade_data.shape, bf16),
            pltpu.VMEM((shards, factors, trades), bf16),
            pltpu.SemaphoreType.DMA((shards,)),
            pltpu.SemaphoreType.DMA((shards,)),
        ],
        compiler_params=params,
        cost_estimate=pl.CostEstimate(
            flops=shards * trades * paths * 2 * 256 * 4,
            bytes_accessed=shards * trades * paths * 2,
            transcendentals=shards * trades * paths,
        ),
    )(weight, trade_data, factor_rows, loss_spanning)


def on_device(
    factors,
    loadings,
    notional,
    strike,
    date_weight,
    loss_spanning,
    loss_local,
    trade_slot,
    span_list,
):
    path_devices = lax.axis_size("path")
    trade_devices = lax.axis_size("trade")
    path_at = lax.axis_index("path")
    trade_at = lax.axis_index("trade")
    dates, factor_count, chunk = factors.shape
    trades = loadings.shape[2]
    group_dates = dates // path_devices
    quarters = trade_devices // group_dates

    first_date = (path_at * group_dates).astype(jnp.int32).reshape(1, 1)
    sent = pack(
        first_date,
        loadings,
        notional,
        strike,
        trade_slot,
        span_list,
        loss_local,
        trade_devices,
        group_dates,
    )
    trade_data = lax.all_to_all(sent, "trade", 0, 0, tiled=True)

    routes = []
    for turn in range(2):
        route = []
        for a in range(path_devices):
            for b in range(trade_devices):
                date = 2 * b + (a + turn) % 2
                to = (date // group_dates) * trade_devices + (date % group_dates) * quarters + a // 2
                route.append((a * trade_devices + b, to))
        routes.append(route)
    mine = lax.dynamic_slice_in_dim(factors, 2 * trade_at, 2, 0)
    odd_path = path_at % 2 == 1
    odd_date = (trade_at // quarters) % 2 == 1
    first = jnp.where(odd_path, mine[1], mine[0])
    second = jnp.where(odd_path, mine[0], mine[1])
    first = lax.ppermute(first, ("path", "trade"), routes[0])
    second = lax.ppermute(second, ("path", "trade"), routes[1])
    factor_rows = jnp.where(
        odd_date,
        jnp.concatenate([second, first], axis=1),
        jnp.concatenate([first, second], axis=1),
    )

    date_at = path_at * group_dates + trade_at // quarters
    weight = lax.dynamic_slice_in_dim(date_weight, date_at, 1).reshape(1, 1)
    loading_part, factor_part = price_and_adjoint(
        weight,
        trade_data,
        factor_rows,
        loss_spanning[None, :],
        trades,
        span_list.shape[0] + loss_local.shape[0],
        1.0 / (path_devices * chunk),
    )
    loading_part = lax.all_to_all(loading_part, "trade", 0, 0, tiled=True)
    back = [[(to, origin) for origin, to in route] for route in routes]
    left, right = factor_part[:, :chunk], factor_part[:, chunk:]
    first = lax.ppermute(jnp.where(odd_date, right, left), ("path", "trade"), back[0])
    second = lax.ppermute(jnp.where(odd_date, left, right), ("path", "trade"), back[1])
    factor_grad = jnp.where(odd_path, jnp.stack([second, first]), jnp.stack([first, second]))

    loading_part = loading_part.reshape(group_dates, quarters, factor_count, trades)
    loading_grad = loading_part.astype(f32).sum(axis=1)
    return (loading_grad, factor_grad)


def solution(mesh):
    return jax.shard_map(
        on_device,
        mesh=mesh,
        in_specs=(
            P(None, None, "path"),
            P(None, None, "trade"),
            P("trade"),
            P("trade"),
            P(),
            P(),
            P("trade"),
            P("trade"),
            P("trade"),
        ),
        out_specs=(P("path", None, "trade"), P("trade", None, "path")),
        check_vma=False,
    )
```

```python
import functools
import math

import jax
import jax.numpy as jnp
from jax import lax
from jax.experimental import pallas as pl
from jax.experimental.pallas import tpu as pltpu
from jax.sharding import PartitionSpec as P

smoothing = 0.5
log2e = math.log2(math.e)
f32 = jnp.float32
bf16 = jnp.bfloat16
nt = (((1,), (1,)), ((), ()))


def split(x):
    high = x.astype(bf16)
    return high, (x - high.astype(f32)).astype(bf16)


def split3(x):
    high, low = split(x)
    return high, low, split(x - high.astype(f32))[1]


def folded(row):
    width = row.shape[1] // 8
    return jnp.concatenate([row[:, at * width : (at + 1) * width] for at in range(8)], axis=0)


def unfolded(block):
    return jnp.concatenate([block[at : at + 1] for at in range(8)], axis=1)


def rows_of(data, trades):
    width = trades // 8
    slot, high, low = (data[:, trades + at * width : trades + (at + 1) * width] for at in range(3))
    return data[:, :trades], unfolded(slot), unfolded(high + low)


def lists_of(data):
    lists = data[:, data.shape[1] - 128 :]
    constant = lists[4:6] + lists[6:8]
    constant = jnp.concatenate([constant[0:1], constant[1:2]], axis=1)
    return lists[0:1], lists[1:2] + lists[2:3] + lists[3:4], constant


def pack_kernel(
    slots, first_ref, loading_ref, notional_ref, strike_ref, slot_ref, span_ref, loss_ref, sent_ref, own_ref, sem
):
    devices = sent_ref.shape[0]
    group_dates = own_ref.shape[0]
    quarters = devices // group_dates
    own = pltpu.make_async_copy(
        loading_ref.at[pl.ds(first_ref[0, 0], group_dates)], own_ref, sem
    )
    own.start()
    trades = notional_ref.shape[1]
    notional = notional_ref[...]
    slot = slot_ref[...].astype(f32)
    amount = notional * (1.0 - strike_ref[...])
    ids = lax.broadcasted_iota(jnp.int32, (slots, trades), 0).astype(f32)
    constant = jnp.where(ids == slot, amount, 0.0).sum(axis=1, keepdims=True)
    constant = jnp.broadcast_to(constant, (slots, 128)).T[0:1]
    lists = [span_ref[...].astype(f32)] + [part.astype(f32) for part in split3(loss_ref[...])]
    for part in split(constant):
        part = part.astype(f32)
        lists += [part[:, : slots // 2], part[:, slots // 2 :]]
    high, low = (part.astype(f32) for part in split(notional))
    extra = [folded(row) for row in (slot, high, low)] + [jnp.concatenate(lists, axis=0)]
    own.wait()
    for date in range(group_dates):
        block = jnp.concatenate([own_ref[date].astype(f32)] + extra, axis=1).astype(bf16)
        for quarter in range(quarters):
            sent_ref[date * quarters + quarter] = block


def table_of(slot, slots):
    ids = lax.broadcasted_iota(jnp.int32, (slots, slot.shape[1]), 0).astype(f32).astype(bf16)
    return jnp.where(ids == slot.astype(bf16), jnp.ones((), bf16), jnp.zeros((), bf16))


def start_all(copy_of, count):
    def start(shard, carry):
        copy_of(shard).start()
        return carry

    lax.fori_loop(0, count, start, 0)


def wait_all(copy_of, count):
    def wait(shard, carry):
        copy_of(shard).wait()
        return carry

    lax.fori_loop(0, count, wait, 0)


def forward_kernel(
    slots,
    weight_ref,
    trade_in,
    row_ref,
    values_out,
    local_out,
    span_out,
    values_ref,
    trade_ref,
    trade_sem,
    values_sem,
):
    shards, paths, trades = values_ref.shape
    span_count = span_out.shape[1]
    span_local = slots - local_out.shape[2]
    weight = weight_ref[0, 0]
    column = jnp.concatenate([row_ref[...].astype(f32)] * 2, axis=0).T.astype(bf16)

    def copy_in(shard):
        return pltpu.make_async_copy(trade_in.at[shard], trade_ref.at[shard], trade_sem.at[shard])

    def copy_out(shard):
        return pltpu.make_async_copy(
            values_ref.at[shard], values_out.at[shard], values_sem.at[shard]
        )

    start_all(copy_in, shards)

    def forward(shard, span_total):
        copy_in(shard).wait()
        data = trade_ref[shard].astype(f32)
        loading, slot, notional = rows_of(data, trades)
        names, loss, constant = lists_of(data)
        both = jnp.concatenate(split(loading * log2e), axis=0)
        exponent = jnp.dot(column, both, preferred_element_type=f32)
        values = (notional * (jnp.exp2(exponent) - 1.0)).astype(bf16)
        values_ref[shard] = values
        copy_out(shard).start()
        partial = constant + lax.dot_general(
            values, table_of(slot, slots), nt, preferred_element_type=f32
        )
        local = weight * loss * jax.nn.sigmoid(partial[:, span_local:] / smoothing)
        local_out[shard] = local.astype(bf16)
        table = table_of(names, span_count)
        for part in split(partial[:, :span_local]):
            span_total = span_total + lax.dot_general(
                part, table, nt, preferred_element_type=f32
            )
        return span_total

    span_out[...] = lax.fori_loop(
        0, shards, forward, jnp.zeros((paths, span_count), f32), unroll=2
    )
    wait_all(copy_out, shards)


def backward_kernel(
    scale,
    weight_ref,
    trade_in,
    row_ref,
    loss_ref,
    span_ref,
    other_ref,
    local_ref,
    values_in,
    loading_out,
    factor_out,
    values_ref,
    trade_ref,
    loading_ref,
    trade_sem,
    values_sem,
    loading_sem,
):
    shards, paths, trades = values_ref.shape
    factors = row_ref.shape[0]
    span_count = loss_ref.shape[1]
    slots = 2 * local_ref.shape[2]
    weight = weight_ref[0, 0]
    row = row_ref[...]

    def copy_in(shard):
        return pltpu.make_async_copy(trade_in.at[shard], trade_ref.at[shard], trade_sem.at[shard])

    def copy_values(shard):
        return pltpu.make_async_copy(
            values_in.at[shard], values_ref.at[shard], values_sem.at[shard]
        )

    def copy_out(shard):
        return pltpu.make_async_copy(
            loading_ref.at[shard], loading_out.at[shard], loading_sem.at[shard]
        )

    start_all(copy_in, shards)
    start_all(copy_values, shards)
    span_total = span_ref[...] + other_ref[...]
    span_weight = (weight * loss_ref[...] * jax.nn.sigmoid(span_total / smoothing)).astype(bf16)

    def backward(shard, total):
        copy_in(shard).wait()
        copy_values(shard).wait()
        data = trade_ref[shard].astype(f32)
        loading, slot, notional = rows_of(data, trades)
        names, _, _ = lists_of(data)
        span_slots = jnp.dot(
            span_weight, table_of(names, span_count), preferred_element_type=f32
        ).astype(bf16)
        slot_weight = jnp.concatenate([span_slots, local_ref[shard]], axis=1)
        trade_weight = jnp.dot(slot_weight, table_of(slot, slots), preferred_element_type=f32)
        scaled = values_ref[shard].astype(f32) + notional
        sensitivity = (trade_weight * scaled).astype(bf16)
        paths_sum = jnp.dot(row, sensitivity, preferred_element_type=f32)
        loading_ref[shard] = (paths_sum * scale).astype(bf16)
        copy_out(shard).start()
        return total + lax.dot_general(
            loading.astype(bf16), sensitivity, nt, preferred_element_type=f32
        )

    factor_out[...] = lax.fori_loop(0, shards, backward, jnp.zeros((factors, paths), f32), unroll=2)
    wait_all(copy_out, shards)


vmem = pl.BlockSpec(memory_space=pltpu.VMEM)
anywhere = pl.BlockSpec(memory_space=pl.ANY)
dma = pltpu.SemaphoreType.DMA
smem = pl.BlockSpec(memory_space=pltpu.SMEM)
params = pltpu.CompilerParams(vmem_limit_bytes=58 * 2**20)


def pack(first, loadings, notional, strike, trade_slot, span_list, loss_local, devices, group_dates):
    factors, trades = loadings.shape[1:]
    slots = span_list.shape[0] + loss_local.shape[0]
    return pl.pallas_call(
        functools.partial(pack_kernel, slots),
        out_shape=jax.ShapeDtypeStruct((devices, factors, trades + 3 * (trades // 8) + 128), bf16),
        in_specs=[smem, anywhere] + [vmem] * 5,
        out_specs=vmem,
        scratch_shapes=[
            pltpu.VMEM((group_dates, factors, trades), bf16),
            pltpu.SemaphoreType.DMA,
        ],
        compiler_params=params,
    )(
        first,
        loadings,
        notional[None],
        strike[None],
        trade_slot[None],
        span_list[None],
        loss_local[None],
    )


def price(weight, trade_data, factor_rows, trades, local_count, slots, span_count):
    shards = trade_data.shape[0]
    paths = factor_rows.shape[1]
    return pl.pallas_call(
        functools.partial(forward_kernel, slots),
        out_shape=(
            jax.ShapeDtypeStruct((shards, paths, trades), bf16),
            jax.ShapeDtypeStruct((shards, paths, local_count), bf16),
            jax.ShapeDtypeStruct((paths, span_count), f32),
        ),
        in_specs=[smem, anywhere, vmem],
        out_specs=(anywhere, vmem, vmem),
        scratch_shapes=[
            pltpu.VMEM((shards, paths, trades), bf16),
            pltpu.VMEM(trade_data.shape, bf16),
            dma((shards,)),
            dma((shards,)),
        ],
        compiler_params=params,
    )(weight, trade_data, factor_rows)


def adjoint(weight, trade_data, factor_rows, loss_spanning, span, other, local, values, scale):
    shards, paths, trades = values.shape
    factors = factor_rows.shape[0]
    return pl.pallas_call(
        functools.partial(backward_kernel, scale),
        out_shape=(
            jax.ShapeDtypeStruct((shards, factors, trades), bf16),
            jax.ShapeDtypeStruct((factors, paths), f32),
        ),
        in_specs=[smem, anywhere] + [vmem] * 5 + [anywhere],
        out_specs=(anywhere, vmem),
        scratch_shapes=[
            pltpu.VMEM(values.shape, bf16),
            pltpu.VMEM(trade_data.shape, bf16),
            pltpu.VMEM((shards, factors, trades), bf16),
            dma((shards,)),
            dma((shards,)),
            dma((shards,)),
        ],
        compiler_params=params,
    )(weight, trade_data, factor_rows, loss_spanning, span, other, local, values)


def on_device(
    factors,
    loadings,
    notional,
    strike,
    date_weight,
    loss_spanning,
    loss_local,
    trade_slot,
    span_list,
):
    path_devices = lax.axis_size("path")
    trade_devices = lax.axis_size("trade")
    path_at = lax.axis_index("path")
    trade_at = lax.axis_index("trade")
    dates, factor_count, chunk = factors.shape
    trades = loadings.shape[2]
    group_dates = dates // path_devices
    columns = trade_devices // 2
    halves = columns // group_dates
    chunks = path_devices // halves
    slots = span_list.shape[0] + loss_local.shape[0]
    sides = [[2 * at + side for at in range(columns)] for side in range(2)]
    partner = [(at, at ^ 1) for at in range(trade_devices)]

    first_date = (path_at * group_dates).astype(jnp.int32).reshape(1, 1)
    sent = pack(
        first_date,
        loadings,
        notional,
        strike,
        trade_slot,
        span_list,
        loss_local,
        columns,
        group_dates,
    )
    trade_data = lax.all_to_all(sent, "trade", 0, 0, axis_index_groups=sides, tiled=True)

    axes = ("path", "trade")
    routes = {}
    for high in range(2):
        for low in range(2):
            route = []
            for a in range(path_devices):
                for b in range(trade_devices):
                    date = 2 * b + (((a // 2) % 2) ^ high)
                    column = (date % group_dates) * halves + a // chunks
                    to = (date // group_dates) * trade_devices + 2 * column + ((a % 2) ^ low)
                    route.append((a * trade_devices + b, to))
            routes[high, low] = route
    mine = lax.dynamic_slice_in_dim(factors, 2 * trade_at, 2, 0)
    odd_pair = (path_at // 2) % 2 == 1
    ready = (
        jnp.where(odd_pair, mine[1], mine[0]),
        jnp.where(odd_pair, mine[0], mine[1]),
    )
    came = {at: lax.ppermute(ready[at[0]], axes, route) for at, route in routes.items()}
    column_at = trade_at // 2
    odd_date = (column_at // halves) % 2 == 1
    odd_core = trade_at % 2 == 1

    def ordered(grid):
        rows = [
            [jnp.where(odd_date, grid[1 - high, low], grid[high, low]) for low in range(2)]
            for high in range(2)
        ]
        return {
            (high, low): jnp.where(odd_core, rows[high][1 - low], rows[high][low])
            for high in range(2)
            for low in range(2)
        }

    places = [(0, 0), (0, 1), (1, 0), (1, 1)]
    grid = ordered(came)
    factor_rows = jnp.concatenate([grid[at] for at in places], axis=1)

    date_at = path_at * group_dates + column_at // halves
    weight = lax.dynamic_slice_in_dim(date_weight, date_at, 1).reshape(1, 1)
    values, local, span = price(
        weight, trade_data, factor_rows, trades, loss_local.shape[0], slots, loss_spanning.shape[0]
    )
    other = lax.ppermute(span, "trade", partner)
    loading_part, factor_part = adjoint(
        weight,
        trade_data,
        factor_rows,
        loss_spanning[None, :],
        span,
        other,
        local,
        values,
        1.0 / (path_devices * chunk),
    )
    loading_part = lax.all_to_all(
        loading_part, "trade", 0, 0, axis_index_groups=sides, tiled=True
    )

    parts = {at: factor_part[:, k * chunk : (k + 1) * chunk] for k, at in enumerate(places)}
    leaving = ordered(parts)
    came = {
        at: lax.ppermute(leaving[at], axes, [(to, origin) for origin, to in route])
        for at, route in routes.items()
    }
    same, opposite = (came[high, 0] + came[high, 1] for high in range(2))
    factor_grad = jnp.where(odd_pair, jnp.stack([opposite, same]), jnp.stack([same, opposite]))

    loading_part = loading_part.reshape(group_dates, halves, factor_count, trades)
    loading_grad = loading_part.astype(f32).sum(axis=1)
    return (loading_grad, factor_grad)


def solution(mesh):
    return jax.shard_map(
        on_device,
        mesh=mesh,
        in_specs=(
            P(None, None, "path"),
            P(None, None, "trade"),
            P("trade"),
            P("trade"),
            P(),
            P(),
            P("trade"),
            P("trade"),
            P("trade"),
        ),
        out_specs=(P("path", None, "trade"), P("trade", None, "path")),
        check_vma=False,
    )
```

```python
import functools
import math

import jax
import jax.numpy as jnp
from jax import lax
from jax.experimental import pallas as pl
from jax.experimental.pallas import tpu as pltpu
from jax.sharding import PartitionSpec as P

smoothing = 0.5
log2e = math.log2(math.e)
f32 = jnp.float32
bf16 = jnp.bfloat16
nt = (((1,), (1,)), ((), ()))


def split(x):
    high = x.astype(bf16)
    return high, (x - high.astype(f32)).astype(bf16)


def split3(x):
    high, low = split(x)
    return high, low, split(x - high.astype(f32))[1]


def folded(row):
    width = row.shape[1] // 8
    return jnp.concatenate([row[:, at * width : (at + 1) * width] for at in range(8)], axis=0)


def unfolded(block):
    return jnp.concatenate([block[at : at + 1] for at in range(8)], axis=1)


def rows_of(data, trades):
    width = trades // 8
    slot, high, low = (data[:, trades + at * width : trades + (at + 1) * width] for at in range(3))
    return data[:, :trades], unfolded(slot), unfolded(high + low)


def lists_of(data):
    lists = data[:, data.shape[1] - 128 :]
    constant = lists[4:6] + lists[6:8]
    constant = jnp.concatenate([constant[0:1], constant[1:2]], axis=1)
    return lists[0:1], lists[1:2] + lists[2:3] + lists[3:4], constant


def pack_kernel(
    slots, first_ref, loading_ref, notional_ref, strike_ref, slot_ref, span_ref, loss_ref, sent_ref, own_ref, sem
):
    devices = sent_ref.shape[0]
    group_dates = own_ref.shape[0]
    quarters = devices // group_dates
    own = pltpu.make_async_copy(
        loading_ref.at[pl.ds(first_ref[0, 0], group_dates)], own_ref, sem
    )
    own.start()
    trades = notional_ref.shape[1]
    notional = notional_ref[...]
    slot = slot_ref[...].astype(f32)
    amount = notional * (1.0 - strike_ref[...])
    ids = lax.broadcasted_iota(jnp.int32, (slots, trades), 0).astype(f32)
    constant = jnp.where(ids == slot, amount, 0.0).sum(axis=1, keepdims=True)
    constant = jnp.broadcast_to(constant, (slots, 128)).T[0:1]
    lists = [span_ref[...].astype(f32)] + [part.astype(f32) for part in split3(loss_ref[...])]
    for part in split(constant):
        part = part.astype(f32)
        lists += [part[:, : slots // 2], part[:, slots // 2 :]]
    high, low = (part.astype(f32) for part in split(notional))
    extra = [folded(row) for row in (slot, high, low)] + [jnp.concatenate(lists, axis=0)]
    own.wait()
    for date in range(group_dates):
        block = jnp.concatenate([own_ref[date].astype(f32)] + extra, axis=1).astype(bf16)
        for quarter in range(quarters):
            sent_ref[date * quarters + quarter] = block


def table_of(slot, slots):
    ids = lax.broadcasted_iota(jnp.int32, (slots, slot.shape[1]), 0).astype(f32).astype(bf16)
    return jnp.where(ids == slot.astype(bf16), jnp.ones((), bf16), jnp.zeros((), bf16))


def kernel(
    scale,
    weight_ref,
    own_in,
    other_in,
    row_ref,
    loss_ref,
    own_out,
    other_out,
    factor_out,
    values_ref,
    slot_weight_ref,
    trade_ref,
    own_ref,
    other_ref,
    trade_sem,
    loading_sem,
):
    shards, _, width = trade_ref.shape
    half = own_ref.shape[0]
    trades = own_ref.shape[2]
    factors, paths = row_ref.shape
    slots = slot_weight_ref.shape[2]
    span_local = slots // 2
    span_count = loss_ref.shape[1]
    weight = weight_ref[0, 0]
    row = row_ref[...]
    column = jnp.concatenate([row.astype(f32)] * 2, axis=0).T.astype(bf16)

    def place(shard):
        return pl.ds(pl.multiple_of(shard * trades, trades), trades)

    def copy_in(source, first, at):
        return pltpu.make_async_copy(
            source.at[at], trade_ref.at[first + at], trade_sem.at[first + at]
        )

    def copy_out(held, target, first, at):
        return pltpu.make_async_copy(held.at[at], target.at[at], loading_sem.at[first + at])

    sources = ((own_in, 0), (other_in, half))
    targets = ((other_ref, other_out, half), (own_ref, own_out, 0))
    for source, first in sources:

        def fetch(at, carry, source=source, first=first):
            copy_in(source, first, at).start()
            return carry

        lax.fori_loop(0, half, fetch, 0)

    def forward(source, first, at, span_total):
        copy_in(source, first, at).wait()
        shard = first + at
        data = trade_ref[shard].astype(f32)
        loading, slot, notional = rows_of(data, trades)
        names, loss, constant = lists_of(data)
        both = jnp.concatenate(split(loading * log2e), axis=0)
        exponent = jnp.dot(column, both, preferred_element_type=f32)
        values = (notional * (jnp.exp2(exponent) - 1.0)).astype(bf16)
        values_ref[:, place(shard)] = values
        partial = constant + lax.dot_general(
            values, table_of(slot, slots), nt, preferred_element_type=f32
        )
        local = weight * loss * jax.nn.sigmoid(partial[:, span_local:] / smoothing)
        slot_weight_ref[shard, :, span_local:] = local.astype(bf16)
        table = table_of(names, span_count)
        for part in split(partial[:, :span_local]):
            span_total = span_total + lax.dot_general(
                part, table, nt, preferred_element_type=f32
            )
        return span_total

    span_total = jnp.zeros((paths, span_count), f32)
    for source, first in sources:
        span_total = lax.fori_loop(
            0, half, functools.partial(forward, source, first), span_total, unroll=2
        )
    span_weight = (weight * loss_ref[...] * jax.nn.sigmoid(span_total / smoothing)).astype(bf16)

    def backward(held, target, first, at, total):
        shard = first + at
        data = trade_ref[shard].astype(f32)
        loading, slot, notional = rows_of(data, trades)
        names, _, _ = lists_of(data)
        slot_weight_ref[shard, :, :span_local] = jnp.dot(
            span_weight, table_of(names, span_count), preferred_element_type=f32
        ).astype(bf16)
        trade_weight = jnp.dot(
            slot_weight_ref[shard], table_of(slot, slots), preferred_element_type=f32
        )
        scaled = values_ref[:, place(shard)].astype(f32) + notional
        sensitivity = (trade_weight * scaled).astype(bf16)
        paths_sum = jnp.dot(row, sensitivity, preferred_element_type=f32)
        held[at] = (paths_sum * scale).astype(held.dtype)
        copy_out(held, target, first, at).start()
        return total + lax.dot_general(
            loading.astype(bf16), sensitivity, nt, preferred_element_type=f32
        )

    total = jnp.zeros((factors, paths), f32)
    for way in targets:
        total = lax.fori_loop(0, half, functools.partial(backward, *way), total)
    factor_out[...] = total
    for way in targets:

        def drain(at, carry, way=way):
            copy_out(*way, at).wait()
            return carry

        lax.fori_loop(0, half, drain, 0)


vmem = pl.BlockSpec(memory_space=pltpu.VMEM)
anywhere = pl.BlockSpec(memory_space=pl.ANY)
smem = pl.BlockSpec(memory_space=pltpu.SMEM)
params = pltpu.CompilerParams(vmem_limit_bytes=58 * 2**20)


def pack(first, loadings, notional, strike, trade_slot, span_list, loss_local, devices, group_dates):
    factors, trades = loadings.shape[1:]
    slots = span_list.shape[0] + loss_local.shape[0]
    return pl.pallas_call(
        functools.partial(pack_kernel, slots),
        out_shape=jax.ShapeDtypeStruct((devices, factors, trades + 3 * (trades // 8) + 128), bf16),
        in_specs=[smem, anywhere] + [vmem] * 5,
        out_specs=vmem,
        scratch_shapes=[
            pltpu.VMEM((group_dates, factors, trades), bf16),
            pltpu.SemaphoreType.DMA,
        ],
        compiler_params=params,
    )(
        first,
        loadings,
        notional[None],
        strike[None],
        trade_slot[None],
        span_list[None],
        loss_local[None],
    )


def price_and_adjoint(weight, own, other, factor_rows, loss_spanning, trades, slots, scale):
    half = own.shape[0]
    shards = 2 * half
    factors, paths = factor_rows.shape
    parts = (((half, factors, trades), f32), ((half, factors, trades), bf16))
    return pl.pallas_call(
        functools.partial(kernel, scale),
        out_shape=tuple(jax.ShapeDtypeStruct(*part) for part in parts)
        + (jax.ShapeDtypeStruct((factors, paths), f32),),
        in_specs=[smem, anywhere, anywhere, vmem, vmem],
        out_specs=(anywhere, anywhere, vmem),
        scratch_shapes=[
            pltpu.VMEM((paths, shards * trades), bf16),
            pltpu.VMEM((shards, paths, slots), bf16),
            pltpu.VMEM((shards,) + own.shape[1:], bf16),
            pltpu.VMEM(*parts[0]),
            pltpu.VMEM(*parts[1]),
            pltpu.SemaphoreType.DMA((shards,)),
            pltpu.SemaphoreType.DMA((shards,)),
        ],
        compiler_params=params,
        cost_estimate=pl.CostEstimate(
            flops=shards * trades * paths * 2 * 256 * 4,
            bytes_accessed=shards * trades * paths * 2,
            transcendentals=shards * trades * paths,
        ),
    )(weight, own, other, factor_rows, loss_spanning)


def on_device(
    factors,
    loadings,
    notional,
    strike,
    date_weight,
    loss_spanning,
    loss_local,
    trade_slot,
    span_list,
):
    path_devices = lax.axis_size("path")
    trade_devices = lax.axis_size("trade")
    path_at = lax.axis_index("path")
    trade_at = lax.axis_index("trade")
    dates, factor_count, chunk = factors.shape
    trades = loadings.shape[2]
    group_dates = dates // path_devices
    quarters = trade_devices // group_dates
    columns = trade_devices // 2
    sides = [[2 * at + side for at in range(columns)] for side in range(2)]
    partner = [(at, at ^ 1) for at in range(trade_devices)]

    first_date = (path_at * group_dates).astype(jnp.int32).reshape(1, 1)
    sent = pack(
        first_date,
        loadings,
        notional,
        strike,
        trade_slot,
        span_list,
        loss_local,
        columns,
        group_dates,
    )

    routes = []
    for turn in range(2):
        route = []
        for a in range(path_devices):
            for b in range(trade_devices):
                date = 2 * b + (a + turn) % 2
                to = (date // group_dates) * trade_devices + (date % group_dates) * quarters + a // 2
                route.append((a * trade_devices + b, to))
        routes.append(route)
    mine = lax.dynamic_slice_in_dim(factors, 2 * trade_at, 2, 0)
    odd_path = path_at % 2 == 1
    odd_date = (trade_at // quarters) % 2 == 1
    first = jnp.where(odd_path, mine[1], mine[0])
    second = jnp.where(odd_path, mine[0], mine[1])
    first = lax.ppermute(first, ("path", "trade"), routes[0])
    second = lax.ppermute(second, ("path", "trade"), routes[1])
    own = lax.all_to_all(sent, "trade", 0, 0, axis_index_groups=sides, tiled=True)
    own, first, second = lax.optimization_barrier((own, first, second))
    other = lax.ppermute(own, "trade", partner)
    factor_rows = jnp.where(
        odd_date,
        jnp.concatenate([second, first], axis=1),
        jnp.concatenate([first, second], axis=1),
    )

    date_at = path_at * group_dates + trade_at // quarters
    weight = lax.dynamic_slice_in_dim(date_weight, date_at, 1).reshape(1, 1)
    own_part, other_part, factor_part = price_and_adjoint(
        weight,
        own,
        other,
        factor_rows,
        loss_spanning[None, :],
        trades,
        span_list.shape[0] + loss_local.shape[0],
        1.0 / (path_devices * chunk),
    )
    passed = lax.ppermute(other_part, "trade", partner)
    loading_part = (own_part + passed.astype(f32)).astype(bf16)
    loading_part, factor_part = lax.optimization_barrier((loading_part, factor_part))
    loading_part = lax.all_to_all(
        loading_part, "trade", 0, 0, axis_index_groups=sides, tiled=True
    )

    back = [[(to, origin) for origin, to in route] for route in routes]
    left, right = factor_part[:, :chunk], factor_part[:, chunk:]
    first = lax.ppermute(jnp.where(odd_date, right, left), ("path", "trade"), back[0])
    second = lax.ppermute(jnp.where(odd_date, left, right), ("path", "trade"), back[1])
    factor_grad = jnp.where(odd_path, jnp.stack([second, first]), jnp.stack([first, second]))

    loading_part = loading_part.reshape(group_dates, columns // group_dates, factor_count, trades)
    loading_grad = loading_part.astype(f32).sum(axis=1)
    return (loading_grad, factor_grad)


def solution(mesh):
    return jax.shard_map(
        on_device,
        mesh=mesh,
        in_specs=(
            P(None, None, "path"),
            P(None, None, "trade"),
            P("trade"),
            P("trade"),
            P(),
            P(),
            P("trade"),
            P("trade"),
            P("trade"),
        ),
        out_specs=(P("path", None, "trade"), P("trade", None, "path")),
        check_vma=False,
    )
```

```python
import functools
import math

import jax
import jax.numpy as jnp
from jax import lax
from jax.experimental import pallas as pl
from jax.experimental.pallas import tpu as pltpu
from jax.sharding import PartitionSpec as P

smoothing = 0.5
log2e = math.log2(math.e)
f32 = jnp.float32
bf16 = jnp.bfloat16
nt = (((1,), (1,)), ((), ()))


def split(x):
    high = x.astype(bf16)
    return high, (x - high.astype(f32)).astype(bf16)


def split3(x):
    high, low = split(x)
    return high, low, split(x - high.astype(f32))[1]


def folded(row):
    width = row.shape[1] // 8
    return jnp.concatenate([row[:, at * width : (at + 1) * width] for at in range(8)], axis=0)


def unfolded(block):
    return jnp.concatenate([block[at : at + 1] for at in range(8)], axis=1)


def rows_of(data, trades):
    width = trades // 8
    slot, high, low = (data[:, trades + at * width : trades + (at + 1) * width] for at in range(3))
    return data[:, :trades], unfolded(slot), unfolded(high + low)


def lists_of(data):
    lists = data[:, data.shape[1] - 128 :]
    constant = lists[4:6] + lists[6:8]
    constant = jnp.concatenate([constant[0:1], constant[1:2]], axis=1)
    return lists[0:1], lists[1:2] + lists[2:3] + lists[3:4], constant


def pack_kernel(
    slots, first_ref, loading_ref, notional_ref, strike_ref, slot_ref, span_ref, loss_ref, sent_ref, own_ref, sem
):
    devices = sent_ref.shape[0]
    group_dates = own_ref.shape[0]
    quarters = devices // group_dates
    own = pltpu.make_async_copy(
        loading_ref.at[pl.ds(first_ref[0, 0], group_dates)], own_ref, sem
    )
    own.start()
    trades = notional_ref.shape[1]
    notional = notional_ref[...]
    slot = slot_ref[...].astype(f32)
    amount = notional * (1.0 - strike_ref[...])
    ids = lax.broadcasted_iota(jnp.int32, (slots, trades), 0).astype(f32)
    constant = jnp.where(ids == slot, amount, 0.0).sum(axis=1, keepdims=True)
    constant = jnp.broadcast_to(constant, (slots, 128)).T[0:1]
    lists = [span_ref[...].astype(f32)] + [part.astype(f32) for part in split3(loss_ref[...])]
    for part in split(constant):
        part = part.astype(f32)
        lists += [part[:, : slots // 2], part[:, slots // 2 :]]
    high, low = (part.astype(f32) for part in split(notional))
    extra = [folded(row) for row in (slot, high, low)] + [jnp.concatenate(lists, axis=0)]
    own.wait()
    for date in range(group_dates):
        block = jnp.concatenate([own_ref[date].astype(f32)] + extra, axis=1).astype(bf16)
        for quarter in range(quarters):
            sent_ref[date * quarters + quarter] = block


def table_of(slot, slots):
    ids = lax.broadcasted_iota(jnp.int32, (slots, slot.shape[1]), 0).astype(f32).astype(bf16)
    return jnp.where(ids == slot.astype(bf16), jnp.ones((), bf16), jnp.zeros((), bf16))


def kernel(
    scale,
    weight_ref,
    own_in,
    other_in,
    row_ref,
    loss_ref,
    own_out,
    other_out,
    factor_out,
    values_ref,
    slot_weight_ref,
    trade_ref,
    own_ref,
    other_ref,
    trade_sem,
    loading_sem,
):
    shards, _, width = trade_ref.shape
    half = own_ref.shape[0]
    trades = own_ref.shape[2]
    factors, paths = row_ref.shape
    slots = slot_weight_ref.shape[2]
    span_local = slots // 2
    span_count = loss_ref.shape[1]
    weight = weight_ref[0, 0]
    row = row_ref[...]
    column = jnp.concatenate([row.astype(f32)] * 2, axis=0).T.astype(bf16)

    def place(shard):
        return pl.ds(pl.multiple_of(shard * trades, trades), trades)

    def copy_in(source, first, at):
        return pltpu.make_async_copy(
            source.at[at], trade_ref.at[first + at], trade_sem.at[first + at]
        )

    def copy_out(held, target, first, at):
        return pltpu.make_async_copy(held.at[at], target.at[at], loading_sem.at[first + at])

    sources = ((own_in, 0), (other_in, half))
    targets = ((other_ref, other_out, half), (own_ref, own_out, 0))
    for source, first in sources:

        def fetch(at, carry, source=source, first=first):
            copy_in(source, first, at).start()
            return carry

        lax.fori_loop(0, half, fetch, 0)

    def forward(source, first, at, span_total):
        copy_in(source, first, at).wait()
        shard = first + at
        data = trade_ref[shard].astype(f32)
        loading, slot, notional = rows_of(data, trades)
        names, loss, constant = lists_of(data)
        both = jnp.concatenate(split(loading * log2e), axis=0)
        exponent = jnp.dot(column, both, preferred_element_type=f32)
        values = (notional * (jnp.exp2(exponent) - 1.0)).astype(bf16)
        values_ref[:, place(shard)] = values
        partial = constant + lax.dot_general(
            values, table_of(slot, slots), nt, preferred_element_type=f32
        )
        local = weight * loss * jax.nn.sigmoid(partial[:, span_local:] / smoothing)
        slot_weight_ref[shard, :, span_local:] = local.astype(bf16)
        table = table_of(names, span_count)
        for part in split(partial[:, :span_local]):
            span_total = span_total + lax.dot_general(
                part, table, nt, preferred_element_type=f32
            )
        return span_total

    span_total = jnp.zeros((paths, span_count), f32)
    for source, first in sources:
        span_total = lax.fori_loop(
            0, half, functools.partial(forward, source, first), span_total, unroll=4
        )
    span_weight = (weight * loss_ref[...] * jax.nn.sigmoid(span_total / smoothing)).astype(bf16)

    def backward(held, target, first, at, total):
        shard = first + at
        data = trade_ref[shard].astype(f32)
        loading, slot, notional = rows_of(data, trades)
        names, _, _ = lists_of(data)
        slot_weight_ref[shard, :, :span_local] = jnp.dot(
            span_weight, table_of(names, span_count), preferred_element_type=f32
        ).astype(bf16)
        trade_weight = jnp.dot(
            slot_weight_ref[shard], table_of(slot, slots), preferred_element_type=f32
        )
        scaled = values_ref[:, place(shard)].astype(f32) + notional
        sensitivity = (trade_weight * scaled).astype(bf16)
        paths_sum = jnp.dot(row, sensitivity, preferred_element_type=f32)
        held[at] = (paths_sum * scale).astype(held.dtype)
        copy_out(held, target, first, at).start()
        return total + lax.dot_general(
            loading.astype(bf16), sensitivity, nt, preferred_element_type=f32
        )

    total = jnp.zeros((factors, paths), f32)
    for way in targets:
        total = lax.fori_loop(0, half, functools.partial(backward, *way), total)
    factor_out[...] = total
    for way in targets:

        def drain(at, carry, way=way):
            copy_out(*way, at).wait()
            return carry

        lax.fori_loop(0, half, drain, 0)


vmem = pl.BlockSpec(memory_space=pltpu.VMEM)
anywhere = pl.BlockSpec(memory_space=pl.ANY)
smem = pl.BlockSpec(memory_space=pltpu.SMEM)
params = pltpu.CompilerParams(vmem_limit_bytes=58 * 2**20)


def pack(first, loadings, notional, strike, trade_slot, span_list, loss_local, devices, group_dates):
    factors, trades = loadings.shape[1:]
    slots = span_list.shape[0] + loss_local.shape[0]
    return pl.pallas_call(
        functools.partial(pack_kernel, slots),
        out_shape=jax.ShapeDtypeStruct((devices, factors, trades + 3 * (trades // 8) + 128), bf16),
        in_specs=[smem, anywhere] + [vmem] * 5,
        out_specs=vmem,
        scratch_shapes=[
            pltpu.VMEM((group_dates, factors, trades), bf16),
            pltpu.SemaphoreType.DMA,
        ],
        compiler_params=params,
    )(
        first,
        loadings,
        notional[None],
        strike[None],
        trade_slot[None],
        span_list[None],
        loss_local[None],
    )


def price_and_adjoint(weight, own, other, factor_rows, loss_spanning, trades, slots, scale):
    half = own.shape[0]
    shards = 2 * half
    factors, paths = factor_rows.shape
    parts = (((half, factors, trades), f32), ((half, factors, trades), bf16))
    return pl.pallas_call(
        functools.partial(kernel, scale),
        out_shape=tuple(jax.ShapeDtypeStruct(*part) for part in parts)
        + (jax.ShapeDtypeStruct((factors, paths), f32),),
        in_specs=[smem, anywhere, anywhere, vmem, vmem],
        out_specs=(anywhere, anywhere, vmem),
        scratch_shapes=[
            pltpu.VMEM((paths, shards * trades), bf16),
            pltpu.VMEM((shards, paths, slots), bf16),
            pltpu.VMEM((shards,) + own.shape[1:], bf16),
            pltpu.VMEM(*parts[0]),
            pltpu.VMEM(*parts[1]),
            pltpu.SemaphoreType.DMA((shards,)),
            pltpu.SemaphoreType.DMA((shards,)),
        ],
        compiler_params=params,
        cost_estimate=pl.CostEstimate(
            flops=shards * trades * paths * 2 * 256 * 4,
            bytes_accessed=shards * trades * paths * 2,
            transcendentals=shards * trades * paths,
        ),
    )(weight, own, other, factor_rows, loss_spanning)


def on_device(
    factors,
    loadings,
    notional,
    strike,
    date_weight,
    loss_spanning,
    loss_local,
    trade_slot,
    span_list,
):
    path_devices = lax.axis_size("path")
    trade_devices = lax.axis_size("trade")
    path_at = lax.axis_index("path")
    trade_at = lax.axis_index("trade")
    dates, factor_count, chunk = factors.shape
    trades = loadings.shape[2]
    group_dates = dates // path_devices
    quarters = trade_devices // group_dates
    columns = trade_devices // 2
    sides = [[2 * at + side for at in range(columns)] for side in range(2)]
    partner = [(at, at ^ 1) for at in range(trade_devices)]

    first_date = (path_at * group_dates).astype(jnp.int32).reshape(1, 1)
    sent = pack(
        first_date,
        loadings,
        notional,
        strike,
        trade_slot,
        span_list,
        loss_local,
        columns,
        group_dates,
    )

    routes = []
    for turn in range(2):
        route = []
        for a in range(path_devices):
            for b in range(trade_devices):
                date = 2 * b + (a + turn) % 2
                to = (date // group_dates) * trade_devices + (date % group_dates) * quarters + a // 2
                route.append((a * trade_devices + b, to))
        routes.append(route)
    mine = lax.dynamic_slice_in_dim(factors, 2 * trade_at, 2, 0)
    odd_path = path_at % 2 == 1
    odd_date = (trade_at // quarters) % 2 == 1
    first = jnp.where(odd_path, mine[1], mine[0])
    second = jnp.where(odd_path, mine[0], mine[1])
    first = lax.ppermute(first, ("path", "trade"), routes[0])
    second = lax.ppermute(second, ("path", "trade"), routes[1])
    own = lax.all_to_all(sent, "trade", 0, 0, axis_index_groups=sides, tiled=True)
    own, first, second = lax.optimization_barrier((own, first, second))
    other = lax.ppermute(own, "trade", partner)
    factor_rows = jnp.where(
        odd_date,
        jnp.concatenate([second, first], axis=1),
        jnp.concatenate([first, second], axis=1),
    )

    date_at = path_at * group_dates + trade_at // quarters
    weight = lax.dynamic_slice_in_dim(date_weight, date_at, 1).reshape(1, 1)
    own_part, other_part, factor_part = price_and_adjoint(
        weight,
        own,
        other,
        factor_rows,
        loss_spanning[None, :],
        trades,
        span_list.shape[0] + loss_local.shape[0],
        1.0 / (path_devices * chunk),
    )
    passed = lax.ppermute(other_part, "trade", partner)
    loading_part = (own_part + passed.astype(f32)).astype(bf16)
    back = [[(to, origin) for origin, to in route] for route in routes]
    left, right = factor_part[:, :chunk], factor_part[:, chunk:]
    first = lax.ppermute(jnp.where(odd_date, right, left), ("path", "trade"), back[0])
    loading_part, second = lax.optimization_barrier((loading_part, jnp.where(odd_date, left, right)))
    loading_part = lax.all_to_all(
        loading_part, "trade", 0, 0, axis_index_groups=sides, tiled=True
    )

    second = lax.ppermute(second, ("path", "trade"), back[1])
    factor_grad = jnp.where(odd_path, jnp.stack([second, first]), jnp.stack([first, second]))

    loading_part = loading_part.reshape(group_dates, columns // group_dates, factor_count, trades)
    loading_grad = loading_part.astype(f32).sum(axis=1)
    return (loading_grad, factor_grad)


def solution(mesh):
    return jax.shard_map(
        on_device,
        mesh=mesh,
        in_specs=(
            P(None, None, "path"),
            P(None, None, "trade"),
            P("trade"),
            P("trade"),
            P(),
            P(),
            P("trade"),
            P("trade"),
            P("trade"),
        ),
        out_specs=(P("path", None, "trade"), P("trade", None, "path")),
        check_vma=False,
    )
```

```python
import functools
import math

import jax
import jax.numpy as jnp
from jax import lax
from jax.experimental import pallas as pl
from jax.experimental.pallas import tpu as pltpu
from jax.sharding import PartitionSpec as P

smoothing = 0.5
log2e = math.log2(math.e)
f32 = jnp.float32
bf16 = jnp.bfloat16
nt = (((1,), (1,)), ((), ()))


def split(x):
    high = x.astype(bf16)
    return high, (x - high.astype(f32)).astype(bf16)


def split3(x):
    high, low = split(x)
    return high, low, split(x - high.astype(f32))[1]


def folded(row):
    width = row.shape[1] // 8
    return jnp.concatenate([row[:, at * width : (at + 1) * width] for at in range(8)], axis=0)


def unfolded(block):
    return jnp.concatenate([block[at : at + 1] for at in range(8)], axis=1)


def rows_of(data, trades):
    width = trades // 8
    slot, high, low = (data[:, trades + at * width : trades + (at + 1) * width] for at in range(3))
    return data[:, :trades], unfolded(slot), unfolded(high + low)


def lists_of(data):
    lists = data[:, data.shape[1] - 128 :]
    constant = lists[4:6] + lists[6:8]
    constant = jnp.concatenate([constant[0:1], constant[1:2]], axis=1)
    return lists[0:1], lists[1:2] + lists[2:3] + lists[3:4], constant


def pack_kernel(
    slots, first_ref, loading_ref, notional_ref, strike_ref, slot_ref, span_ref, loss_ref, sent_ref, own_ref, sem
):
    devices = sent_ref.shape[0]
    group_dates = own_ref.shape[0]
    quarters = devices // group_dates
    own = pltpu.make_async_copy(
        loading_ref.at[pl.ds(first_ref[0, 0], group_dates)], own_ref, sem
    )
    own.start()
    trades = notional_ref.shape[1]
    notional = notional_ref[...]
    slot = slot_ref[...].astype(f32)
    amount = notional * (1.0 - strike_ref[...])
    ids = lax.broadcasted_iota(jnp.int32, (slots, trades), 0).astype(f32)
    constant = jnp.where(ids == slot, amount, 0.0).sum(axis=1, keepdims=True)
    constant = jnp.broadcast_to(constant, (slots, 128)).T[0:1]
    lists = [span_ref[...].astype(f32)] + [part.astype(f32) for part in split3(loss_ref[...])]
    for part in split(constant):
        part = part.astype(f32)
        lists += [part[:, : slots // 2], part[:, slots // 2 :]]
    high, low = (part.astype(f32) for part in split(notional))
    extra = [folded(row) for row in (slot, high, low)] + [jnp.concatenate(lists, axis=0)]
    own.wait()
    for date in range(group_dates):
        block = jnp.concatenate([own_ref[date].astype(f32)] + extra, axis=1).astype(bf16)
        for quarter in range(quarters):
            sent_ref[date * quarters + quarter] = block


def table_of(slot, slots):
    ids = lax.broadcasted_iota(jnp.int32, (slots, slot.shape[1]), 0).astype(f32).astype(bf16)
    return jnp.where(ids == slot.astype(bf16), jnp.ones((), bf16), jnp.zeros((), bf16))


def kernel(
    scale,
    weight_ref,
    own_in,
    other_in,
    row_ref,
    loss_ref,
    own_out,
    other_out,
    factor_out,
    values_ref,
    slot_weight_ref,
    trade_ref,
    own_ref,
    other_ref,
    trade_sem,
    loading_sem,
):
    shards, _, width = trade_ref.shape
    half = own_ref.shape[0]
    trades = own_ref.shape[2]
    factors, paths = row_ref.shape
    slots = slot_weight_ref.shape[2]
    span_local = slots // 2
    span_count = loss_ref.shape[1]
    weight = weight_ref[0, 0]
    row = row_ref[...]
    column = jnp.concatenate([row.astype(f32)] * 2, axis=0).T.astype(bf16)

    def place(shard):
        return pl.ds(pl.multiple_of(shard * trades, trades), trades)

    def copy_in(source, first, at):
        return pltpu.make_async_copy(
            source.at[at], trade_ref.at[first + at], trade_sem.at[first + at]
        )

    def copy_out(held, target, first, at):
        return pltpu.make_async_copy(held.at[at], target.at[at], loading_sem.at[first + at])

    sources = ((own_in, 0), (other_in, half))
    targets = ((other_ref, other_out, half), (own_ref, own_out, 0))
    for source, first in sources:

        def fetch(at, carry, source=source, first=first):
            copy_in(source, first, at).start()
            return carry

        lax.fori_loop(0, half, fetch, 0)

    def forward(source, first, at, span_total):
        copy_in(source, first, at).wait()
        shard = first + at
        data = trade_ref[shard].astype(f32)
        loading, slot, notional = rows_of(data, trades)
        names, loss, constant = lists_of(data)
        both = jnp.concatenate(split(loading * log2e), axis=0)
        exponent = jnp.dot(column, both, preferred_element_type=f32)
        values = (notional * (jnp.exp2(exponent) - 1.0)).astype(bf16)
        values_ref[:, place(shard)] = values
        partial = constant + lax.dot_general(
            values, table_of(slot, slots), nt, preferred_element_type=f32
        )
        local = weight * loss * jax.nn.sigmoid(partial[:, span_local:] / smoothing)
        slot_weight_ref[shard, :, span_local:] = local.astype(bf16)
        table = table_of(names, span_count)
        for part in split(partial[:, :span_local]):
            span_total = span_total + lax.dot_general(
                part, table, nt, preferred_element_type=f32
            )
        return span_total

    span_total = jnp.zeros((paths, span_count), f32)
    for source, first in sources:
        span_total = lax.fori_loop(
            0, half, functools.partial(forward, source, first), span_total, unroll=4
        )
    span_weight = (weight * loss_ref[...] * jax.nn.sigmoid(span_total / smoothing)).astype(bf16)

    def backward(held, target, first, at, total):
        shard = first + at
        data = trade_ref[shard].astype(f32)
        loading, slot, notional = rows_of(data, trades)
        names, _, _ = lists_of(data)
        slot_weight_ref[shard, :, :span_local] = jnp.dot(
            span_weight, table_of(names, span_count), preferred_element_type=f32
        ).astype(bf16)
        trade_weight = jnp.dot(
            slot_weight_ref[shard], table_of(slot, slots), preferred_element_type=f32
        )
        scaled = values_ref[:, place(shard)].astype(f32) + notional
        sensitivity = (trade_weight * scaled).astype(bf16)
        paths_sum = jnp.dot(row, sensitivity, preferred_element_type=f32)
        held[at] = (paths_sum * scale).astype(held.dtype)
        copy_out(held, target, first, at).start()
        return total + lax.dot_general(
            loading.astype(bf16), sensitivity, nt, preferred_element_type=f32
        )

    total = jnp.zeros((factors, paths), f32)
    for way in targets:
        total = lax.fori_loop(0, half, functools.partial(backward, *way), total)
    factor_out[...] = total
    for way in targets:

        def drain(at, carry, way=way):
            copy_out(*way, at).wait()
            return carry

        lax.fori_loop(0, half, drain, 0)


vmem = pl.BlockSpec(memory_space=pltpu.VMEM)
anywhere = pl.BlockSpec(memory_space=pl.ANY)
smem = pl.BlockSpec(memory_space=pltpu.SMEM)
wide = pltpu.CompilerParams(vmem_limit_bytes=58 * 2**20)
narrow = pltpu.CompilerParams(vmem_limit_bytes=46 * 2**20)


def pack(first, loadings, notional, strike, trade_slot, span_list, loss_local, devices, group_dates):
    factors, trades = loadings.shape[1:]
    slots = span_list.shape[0] + loss_local.shape[0]
    return pl.pallas_call(
        functools.partial(pack_kernel, slots),
        out_shape=jax.ShapeDtypeStruct((devices, factors, trades + 3 * (trades // 8) + 128), bf16),
        in_specs=[smem, anywhere] + [vmem] * 5,
        out_specs=vmem,
        scratch_shapes=[
            pltpu.VMEM((group_dates, factors, trades), bf16),
            pltpu.SemaphoreType.DMA,
        ],
        compiler_params=wide,
    )(
        first,
        loadings,
        notional[None],
        strike[None],
        trade_slot[None],
        span_list[None],
        loss_local[None],
    )


def price_and_adjoint(weight, own, other, factor_rows, loss_spanning, trades, slots, scale):
    half = own.shape[0]
    shards = 2 * half
    factors, paths = factor_rows.shape
    parts = (((half, factors, trades), f32), ((half, factors, trades), bf16))
    return pl.pallas_call(
        functools.partial(kernel, scale),
        out_shape=tuple(jax.ShapeDtypeStruct(*part) for part in parts)
        + (jax.ShapeDtypeStruct((factors, paths), f32),),
        in_specs=[smem, anywhere, anywhere, vmem, vmem],
        out_specs=(anywhere, anywhere, vmem),
        scratch_shapes=[
            pltpu.VMEM((paths, shards * trades), bf16),
            pltpu.VMEM((shards, paths, slots), bf16),
            pltpu.VMEM((shards,) + own.shape[1:], bf16),
            pltpu.VMEM(*parts[0]),
            pltpu.VMEM(*parts[1]),
            pltpu.SemaphoreType.DMA((shards,)),
            pltpu.SemaphoreType.DMA((shards,)),
        ],
        compiler_params=narrow,
        cost_estimate=pl.CostEstimate(
            flops=shards * trades * paths * 2 * 256 * 4,
            bytes_accessed=shards * trades * paths * 2,
            transcendentals=shards * trades * paths,
        ),
    )(weight, own, other, factor_rows, loss_spanning)


def on_device(
    factors,
    loadings,
    notional,
    strike,
    date_weight,
    loss_spanning,
    loss_local,
    trade_slot,
    span_list,
):
    path_devices = lax.axis_size("path")
    trade_devices = lax.axis_size("trade")
    path_at = lax.axis_index("path")
    trade_at = lax.axis_index("trade")
    dates, factor_count, chunk = factors.shape
    trades = loadings.shape[2]
    group_dates = dates // path_devices
    quarters = trade_devices // group_dates
    columns = trade_devices // 2
    sides = [[2 * at + side for at in range(columns)] for side in range(2)]
    partner = [(at, at ^ 1) for at in range(trade_devices)]

    first_date = (path_at * group_dates).astype(jnp.int32).reshape(1, 1)
    sent = pack(
        first_date,
        loadings,
        notional,
        strike,
        trade_slot,
        span_list,
        loss_local,
        columns,
        group_dates,
    )

    routes = []
    for turn in range(2):
        route = []
        for a in range(path_devices):
            for b in range(trade_devices):
                date = 2 * b + (a + turn) % 2
                to = (date // group_dates) * trade_devices + (date % group_dates) * quarters + a // 2
                route.append((a * trade_devices + b, to))
        routes.append(route)
    mine = lax.dynamic_slice_in_dim(factors, 2 * trade_at, 2, 0)
    odd_path = path_at % 2 == 1
    odd_date = (trade_at // quarters) % 2 == 1
    first = jnp.where(odd_path, mine[1], mine[0])
    second = jnp.where(odd_path, mine[0], mine[1])
    first = lax.ppermute(first, ("path", "trade"), routes[0])
    second = lax.ppermute(second, ("path", "trade"), routes[1])
    own = lax.all_to_all(sent, "trade", 0, 0, axis_index_groups=sides, tiled=True)
    own, first, second = lax.optimization_barrier((own, first, second))
    other = lax.ppermute(own, "trade", partner)
    factor_rows = jnp.where(
        odd_date,
        jnp.concatenate([second, first], axis=1),
        jnp.concatenate([first, second], axis=1),
    )

    date_at = path_at * group_dates + trade_at // quarters
    weight = lax.dynamic_slice_in_dim(date_weight, date_at, 1).reshape(1, 1)
    own_part, other_part, factor_part = price_and_adjoint(
        weight,
        own,
        other,
        factor_rows,
        loss_spanning[None, :],
        trades,
        span_list.shape[0] + loss_local.shape[0],
        1.0 / (path_devices * chunk),
    )
    passed = lax.ppermute(other_part, "trade", partner)
    loading_part = (own_part + passed.astype(f32)).astype(bf16)
    back = [[(to, origin) for origin, to in route] for route in routes]
    left, right = factor_part[:, :chunk], factor_part[:, chunk:]
    first = lax.ppermute(jnp.where(odd_date, right, left), ("path", "trade"), back[0])
    loading_part, second = lax.optimization_barrier((loading_part, jnp.where(odd_date, left, right)))
    loading_part = lax.all_to_all(
        loading_part, "trade", 0, 0, axis_index_groups=sides, tiled=True
    )

    second = lax.ppermute(second, ("path", "trade"), back[1])
    factor_grad = jnp.where(odd_path, jnp.stack([second, first]), jnp.stack([first, second]))

    loading_part = loading_part.reshape(group_dates, columns // group_dates, factor_count, trades)
    loading_grad = loading_part.astype(f32).sum(axis=1)
    return (loading_grad, factor_grad)


def solution(mesh):
    return jax.shard_map(
        on_device,
        mesh=mesh,
        in_specs=(
            P(None, None, "path"),
            P(None, None, "trade"),
            P("trade"),
            P("trade"),
            P(),
            P(),
            P("trade"),
            P("trade"),
            P("trade"),
        ),
        out_specs=(P("path", None, "trade"), P("trade", None, "path")),
        check_vma=False,
    )
```
